256 devices in a mesh: rows: 16 (over x, y), leaf: 16 (over z, core).
Axes of the slice: x: 4, y: 4, z: 8, core: 2. Of those that a mesh axis runs over, the one named last changes fastest.
Arguments:
- right_side: float32 [131072, 128], P(('rows', 'leaf')), may hold values from -6 to 6
- reflectors: float32 [131072, 2048], P(('rows', 'leaf')), may hold values from -0.0625 to 0.0625
- leaf_factor: float32 [16, 2048, 2048], P('rows', None, 'leaf'), may hold values from -1 to 1, as said below
- node_reflect: float32 [16, 2048, 2048], P('rows', 'leaf'), may hold values from -0.125 to 0.125
- node_factor: float32 [16, 2048, 2048], P('rows', None, 'leaf'), may hold values from -1 to 1, as said below
- upper_blocks: float32 [2048, 2048], P('leaf'), may hold values from -1 to 1, as said below
- block_inverse: float32 [2048, 128], P('leaf'), may hold values from -2 to 2, as said below
Outputs:
- rotated: float32 [131072, 128], P(('rows', 'leaf'))
- solution: float32 [2048, 128], P('leaf', 'rows')
The draws below stay inside these ranges and needn't reach their ends.
Inputs may be any that keep to these rules, and one draw needn't show every extreme that they name: `leaf_factor`: each [2048, 2048] slot is upper triangular, with diagonal between 0.5 and 1. `node_factor`: each [2048, 2048] slot is upper triangular, with diagonal between 0.5 and 1. `upper_blocks`: zero in every 128 x 128 block on or below the block diagonal. `block_inverse`: each stacked 128 x 128 block is upper triangular, with positive diagonal.
All inputs are finite; a program needn't handle non-finite values.
Results may differ from the reference program's by a relative error of at most 0.0003.
Values sent between devices are 32-bit elements; how exact they have to be, the bound alone decides.
No kernel may reach another device: no remote copies, remote signals or barrier semaphores. Data moves between devices by JAX's collectives and lax.ppermute only.
A program may use at most 128 MiB of HBM per device.

```python
import jax
import jax.numpy as jnp
from jax import lax

ORDER = 2048
RHS = 128
ROWS_DEV = 512
BLOCK = 128
LEAVES = 16
LEAF_ROWS = 8192
TOTAL_ROWS = 131072
N_LEAF = 16


def triangle_factor(key, count, order, off_scale):
    diag_key, off_key = jax.random.split(key)
    diagonal = jax.random.uniform(diag_key, (count, order), jnp.float32, 0.5, 1.0)
    values = jax.random.normal(off_key, (count, order, order), jnp.float32) * off_scale
    row_ids = jnp.arange(order)[:, None]
    col_ids = jnp.arange(order)[None, :]
    strict = col_ids > row_ids
    on_diagonal = col_ids == row_ids
    return jnp.where(strict, values, 0.0) + jnp.where(on_diagonal, 1.0, 0.0) * diagonal[:, :, None]


def draw_leaf_factor(key, part):
    key = jax.random.fold_in(key, 1)
    return triangle_factor(key, LEAVES, ORDER, 0.3 / ORDER ** 0.5)


def draw_node_factor(key, part):
    key = jax.random.fold_in(key, 2)
    return triangle_factor(key, LEAVES, ORDER, 0.3 / ORDER ** 0.5)


def draw_upper_blocks(key, part):
    key = jax.random.fold_in(key, 3)
    values = jax.random.normal(key, (ORDER, ORDER), jnp.float32) * (0.5 / ORDER ** 0.5)
    row_block = jnp.arange(ORDER)[:, None] // BLOCK
    col_block = jnp.arange(ORDER)[None, :] // BLOCK
    return jnp.where(col_block > row_block, values, 0.0)


def draw_block_inverse(key, part):
    key = jax.random.fold_in(key, 4)
    diag_key, off_key = jax.random.split(key)
    diagonal = jnp.exp(jax.random.uniform(diag_key, (ORDER, 1), jnp.float32, -0.69, 0.69))
    values = jax.random.normal(off_key, (ORDER, BLOCK), jnp.float32) * (0.3 / BLOCK ** 0.5)
    local_row = jnp.arange(ORDER)[:, None] % BLOCK
    col_ids = jnp.arange(BLOCK)[None, :]
    return jnp.where(col_ids > local_row, values, 0.0) + jnp.where(col_ids == local_row, diagonal, 0.0)


def block_scale(stream_key, extent, cuts, low, high):
    level, own = 1.0, jax.random.fold_in(stream_key, 6)
    for dim, blocks in cuts:
        draws = jnp.exp(jax.random.uniform(jax.random.fold_in(own, dim), (blocks,), jnp.float32, low / len(cuts), high / len(cuts)))
        level = level * jnp.repeat(draws, extent[dim] // blocks).reshape([-1 if axis == dim else 1 for axis in range(len(extent))])
    return level


def normal_values(key, shape, width, limit, cuts=(), kind=jnp.bfloat16):
    array = width * jax.random.normal(key, shape, jnp.float32)
    if cuts:
        array = array * block_scale(key, shape, cuts, -0.22, 0.18)
    return jnp.clip(array, -limit, limit).astype(kind)


def setup_inputs(seed: int = 0) -> dict:
    splits = jax.random.split(jax.random.key(seed), 8)
    right_side = normal_values(splits[0], (TOTAL_ROWS, RHS), 1.0, 6.0, ((0, 256),), jnp.float32)
    reflectors = normal_values(splits[1], (TOTAL_ROWS, ORDER), LEAF_ROWS ** -0.5, 0.0625, ((0, 256),), jnp.float32)
    leaf_factor = draw_leaf_factor(jax.random.fold_in(splits[7], 71), 0)
    node_reflect = normal_values(splits[3], (LEAVES, ORDER, ORDER), ORDER ** -0.5, 0.125, ((0, 16), (1, 16)), jnp.float32)
    node_factor = draw_node_factor(jax.random.fold_in(splits[7], 71), 0)
    upper_blocks = draw_upper_blocks(jax.random.fold_in(splits[7], 71), 0)
    block_inverse = draw_block_inverse(jax.random.fold_in(splits[7], 71), 0)
    return {"right_side": right_side, "reflectors": reflectors, "leaf_factor": leaf_factor, "node_reflect": node_reflect, "node_factor": node_factor, "upper_blocks": upper_blocks, "block_inverse": block_inverse}


highest = lax.Precision.HIGHEST


def product(left, right):
    return jnp.dot(left, right, precision=highest, preferred_element_type=jnp.float32)


def reference(right_side, reflectors, leaf_factor, node_reflect, node_factor, upper_blocks, block_inverse):
    def leaf_apply(pieces):
        side, vectors, factor = pieces
        weights = product(vectors.T, side)
        coeffs = product(factor.T, weights)
        return side - product(vectors, coeffs)

    leaves_out = lax.map(leaf_apply, (right_side.reshape(LEAVES, LEAF_ROWS, RHS), reflectors.reshape(LEAVES, LEAF_ROWS, ORDER), leaf_factor))
    leaves_out = leaves_out.reshape(LEAVES, N_LEAF, ROWS_DEV, RHS)
    summits = [leaves_out[index, :, :BLOCK].reshape(ORDER, RHS) for index in range(LEAVES)]
    stride = 1
    while stride < LEAVES:
        for lower_row in range(0, LEAVES, 2 * stride):
            upper_row = lower_row + stride
            lower_top = summits[lower_row]
            upper_top = summits[upper_row]
            lower_part = node_reflect[upper_row]
            combined = lower_top + product(lower_part.T, upper_top)
            coeffs = product(node_factor[upper_row].T, combined)
            summits[lower_row] = lower_top - coeffs
            summits[upper_row] = upper_top - product(lower_part, coeffs)
        stride = stride * 2
    new_tops = jnp.stack(summits).reshape(LEAVES, N_LEAF, BLOCK, RHS)
    rotated = jnp.concatenate([new_tops, leaves_out[:, :, BLOCK:]], axis=2).reshape(TOTAL_ROWS, RHS)
    root_top = summits[0]
    solution = jnp.zeros((ORDER, RHS), jnp.float32)
    for target in reversed(range(N_LEAF)):
        first_row = target * BLOCK
        band = upper_blocks[first_row:first_row + BLOCK]
        remainder = root_top[first_row:first_row + BLOCK] - product(band, solution)
        value = product(block_inverse[first_row:first_row + BLOCK], remainder)
        solution = solution.at[first_row:first_row + BLOCK].set(value)
    return rotated, solution
```

```python
import jax
import jax.numpy as jnp
from jax import lax
from jax.sharding import PartitionSpec as P

high = lax.Precision.HIGH
highest = lax.Precision.HIGHEST


def dot(left, right, contract, precision=high):
    return lax.dot_general(
        left, right, (contract, ((), ())), precision=precision, preferred_element_type=jnp.float32
    )


def moved(value, axis, pairs):
    return lax.ppermute(value, axis, pairs)


def per_device(
    right_side, reflectors, leaf_factor, node_reflect, node_factor, upper_blocks, block_inverse
):
    block = upper_blocks.shape[0]
    columns = right_side.shape[1]
    count = lax.axis_size("leaf")
    rows = lax.axis_size("rows")
    half = count // 2
    row_index = lax.axis_index("rows")
    leaf_index = lax.axis_index("leaf")
    parity = leaf_index % 2
    swap = [(i, i ^ 1) for i in range(count)]
    same = [list(range(k, count, 2)) for k in range(2)]

    def scatter_sum(partial):
        parts = partial.reshape(columns, half, 2, block).transpose(2, 1, 0, 3)
        keep = lax.dynamic_index_in_dim(parts, parity, 0, keepdims=False)
        give = lax.dynamic_index_in_dim(parts, 1 - parity, 0, keepdims=False)
        pair = keep + moved(give, "leaf", swap)
        got = lax.all_to_all(pair, "leaf", 0, 0, axis_index_groups=same)
        return jnp.sum(got, axis=0)

    def collect(mine):
        spread = jnp.broadcast_to(mine[None], (half,) + mine.shape)
        own = lax.all_to_all(spread, "leaf", 0, 0, axis_index_groups=same)
        other = moved(own, "leaf", swap)
        even = jnp.where(parity == 0, own, other)
        odd = jnp.where(parity == 0, other, own)
        whole = jnp.stack([even, odd], axis=1)
        return whole.transpose(2, 0, 1, 3).reshape(mine.shape[0], count * block)

    factor_whole = lax.all_gather(node_factor[0], "leaf", axis=0)
    upper_whole = lax.all_gather(upper_blocks, "leaf", axis=0, tiled=True)
    inverse_whole = lax.all_gather(block_inverse, "leaf", axis=0)

    weights_part = scatter_sum(dot(right_side, reflectors, ((0,), (0,))))
    weights = collect(weights_part)
    coeffs = collect(dot(weights, leaf_factor[0], ((1,), (0,))))
    rotated = right_side - dot(reflectors, coeffs, ((1,), (1,)))
    top = rotated[:block].T

    reflect_factor = jnp.einsum(
        "ij,kjl->ikl", node_reflect[0], factor_whole, precision=high,
        preferred_element_type=jnp.float32,
    ).reshape(block, count * block)
    factor_rows = lax.dynamic_slice_in_dim(factor_whole, leaf_index * block, block, 1)
    factor_rows = factor_rows.transpose(1, 0, 2).reshape(block, count * block)
    joint = jnp.concatenate([reflect_factor, factor_rows], axis=0)

    stride = 1
    upper = top
    lower = moved(top, "rows", [(i, i + 1) for i in range(0, rows, 2)])
    own_coeffs = jnp.zeros_like(top)
    own_top = top
    while stride < rows:
        if stride > 1:
            nodes = list(range(stride, rows, 2 * stride))
            upper = moved(lower, "rows", [(j + stride // 2, j) for j in nodes])
            lower = moved(lower, "rows", [(j - stride // 2, j) for j in nodes])
        share = scatter_sum(dot(jnp.concatenate([upper, lower], axis=1), joint, ((1,), (0,))))
        lower = lower - share
        mine = row_index % (2 * stride) == stride
        own_coeffs = jnp.where(mine, share, own_coeffs)
        own_top = jnp.where(mine, upper, own_top)
        stride *= 2
    root = rows // 2

    pieces = lower.reshape(rows, columns // rows, block)
    arrived = lax.all_to_all(pieces, "rows", 0, 0)[root]
    spread = jnp.broadcast_to(arrived[None], (count,) + arrived.shape)
    right = lax.all_to_all(spread, "leaf", 0, 0)

    back = moved(lower, "rows", [(root, 0)])
    all_coeffs = collect(own_coeffs)
    lowered = own_top - dot(all_coeffs, node_reflect[0], ((1,), (1,)))
    final_top = jnp.where(row_index == 0, back, lowered)
    rotated = jnp.concatenate([final_top.T, rotated[block:]], axis=0)

    blocks = [right[k] for k in range(count)]
    solved = None
    for k in reversed(range(count)):
        remainder = blocks[k]
        if solved is not None:
            band = upper_whole[k * block:(k + 1) * block, (k + 1) * block:]
            remainder = remainder - dot(solved, band, ((1,), (1,)), highest)
        value = dot(remainder, inverse_whole[k], ((1,), (1,)), highest)
        solved = value if solved is None else jnp.concatenate([value, solved], axis=1)
    solution = lax.dynamic_slice_in_dim(solved, leaf_index * block, block, 1).T
    return (rotated, solution)


def solution(mesh):
    in_specs = (
        P(("rows", "leaf"), None),
        P(("rows", "leaf"), None),
        P("rows", None, "leaf"),
        P("rows", "leaf", None),
        P("rows", None, "leaf"),
        P("leaf", None),
        P("leaf", None),
    )
    out_specs = (P(("rows", "leaf"), None), P("leaf", "rows"))
    return jax.shard_map(
        per_device, mesh=mesh, in_specs=in_specs, out_specs=out_specs, check_vma=False
    )
```

```python
import functools

import jax
import jax.numpy as jnp
from jax import lax
from jax.experimental import pallas as pl
from jax.experimental.pallas import tpu as pltpu
from jax.sharding import PartitionSpec as P

SIDE = 128
SPLIT = (((1,), (0,)), ((), ()))
LIMIT = 56 * 1024 * 1024


def halves(value):
    high = value.astype(jnp.bfloat16)
    low = (value - high.astype(jnp.float32)).astype(jnp.bfloat16)
    return high, low


def once(left, right):
    return lax.dot_general(left, right, SPLIT, preferred_element_type=jnp.float32)


def thrice(left, right):
    return once(left[0], right[0]) + (once(left[0], right[1]) + once(left[1], right[0]))


def full(left, right):
    return lax.dot_general(
        left, right, SPLIT, precision=lax.Precision.HIGHEST, preferred_element_type=jnp.float32
    )


def pick(parity, own, other):
    first = parity == 0
    return jnp.where(first, own, other), jnp.where(first, other, own)


smem = pl.BlockSpec(memory_space=pltpu.SMEM)


def params():
    return pltpu.CompilerParams(vmem_limit_bytes=LIMIT)


def shaped(*shape, dtype=jnp.float32):
    return jax.ShapeDtypeStruct(shape, dtype)


def weights_kernel(where_ref, side_ref, vectors_ref, keep_ref, give_ref, high_ref, low_ref):
    @pl.when(pl.program_id(0) == 0)
    def _():
        high, low = halves(side_ref[...].T)
        high_ref[...] = high
        low_ref[...] = low

    out = thrice((high_ref[...], low_ref[...]), halves(vectors_ref[...]))
    first = where_ref[0] == 0
    even, odd = out[:, :SIDE], out[:, SIDE:]
    keep_ref[0] = jnp.where(first, even, odd)
    give_ref[0] = jnp.where(first, odd, even)


def weights_of(where, side, vectors):
    tall, order = vectors.shape
    columns = side.shape[1]
    steps = order // (2 * SIDE)
    block = pl.BlockSpec((1, columns, SIDE), lambda n: (n, 0, 0))
    return pl.pallas_call(
        weights_kernel,
        grid=(steps,),
        in_specs=[
            smem,
            pl.BlockSpec((tall, columns), lambda n: (0, 0)),
            pl.BlockSpec((tall, 2 * SIDE), lambda n: (0, n)),
        ],
        out_specs=[block, block],
        out_shape=[shaped(steps, columns, SIDE)] * 2,
        scratch_shapes=[pltpu.VMEM((columns, tall), jnp.bfloat16)] * 2,
        compiler_params=params(),
        name="weights",
    )(where, side, vectors)


def coeffs_kernel(where_ref, own_ref, other_ref, factor_ref, out_ref):
    parity = where_ref[0]
    steps = own_ref.shape[0]
    total = jnp.zeros(own_ref.shape[1:], jnp.float32)
    for n in range(steps):
        left = jnp.concatenate(pick(parity, own_ref[n], other_ref[n]), axis=1)
        right = factor_ref[2 * n * SIDE:(2 * n + 2) * SIDE, :]
        total = total + thrice(halves(left), halves(right))
    total = total.T
    for n in range(steps):
        out_ref[n] = total


def coeffs_of(where, own, other, factor):
    return pl.pallas_call(
        coeffs_kernel,
        in_specs=[smem] + [pl.BlockSpec(memory_space=pltpu.VMEM)] * 3,
        out_shape=shaped(own.shape[0], SIDE, own.shape[1]),
        compiler_params=params(),
        name="coeffs",
    )(where, own, other, factor)


def lowered_kernel(where_ref, own_ref, other_ref, vectors_ref, side_ref, out_ref, top_ref):
    step = pl.program_id(0)

    @pl.when(step == 0)
    def _():
        out_ref[...] = side_ref[...]

    right = jnp.concatenate(pick(where_ref[0], own_ref[0], other_ref[0]), axis=0)
    out_ref[...] -= thrice(halves(vectors_ref[...]), halves(right))

    @pl.when(step == pl.num_programs(0) - 1)
    def _():
        top_ref[...] = out_ref[:SIDE, :].T


def lowered_of(where, own, other, vectors, side):
    tall, order = vectors.shape
    columns = side.shape[1]
    steps = order // (2 * SIDE)
    block = pl.BlockSpec((1, SIDE, columns), lambda n: (n, 0, 0))
    whole = pl.BlockSpec((tall, columns), lambda n: (0, 0))
    return pl.pallas_call(
        lowered_kernel,
        grid=(steps,),
        in_specs=[smem, block, block, pl.BlockSpec((tall, 2 * SIDE), lambda n: (0, n)), whole],
        out_specs=[whole, pl.BlockSpec((columns, SIDE), lambda n: (0, 0))],
        out_shape=[shaped(tall, columns), shaped(columns, SIDE)],
        compiler_params=params(),
        name="lowered",
    )(where, own, other, vectors, side)


def joint_kernel(where_ref, reflect_ref, short_ref, long_ref, *refs):
    out_refs, scratch = refs[:4], refs[4:]
    reflect_high, reflect_low, panel_high, panel_low, panel = scratch
    step = pl.program_id(0)
    kept = short_ref.shape[1]
    order = reflect_ref.shape[1]

    @pl.when(step == 0)
    def _():
        high, low = halves(reflect_ref[...])
        reflect_high[...] = high
        reflect_low[...] = low

    edge = (step + 1) * SIDE
    row = lax.broadcasted_iota(jnp.int32, (kept, SIDE), 0)
    panel[:, :SIDE] = jnp.zeros((order, SIDE), jnp.float32)
    panel[0:kept, :SIDE] = jnp.where(row < edge, short_ref[0], 0.0)
    panel[0:kept, SIDE:] = long_ref[0]
    rest = order - kept
    start = pl.multiple_of(edge, SIDE)
    tail = short_ref[0, pl.ds(jnp.minimum(start, kept - SIDE), SIDE), :]
    for n in range(rest // SIDE):
        at = pl.multiple_of(jnp.minimum(edge + n * SIDE, kept - SIDE), SIDE)
        piece = short_ref[0, pl.ds(at, SIDE), :]
        inside = edge + n * SIDE < kept - SIDE
        panel[kept + n * SIDE:kept + (n + 1) * SIDE, SIDE:] = jnp.where(inside, piece, 0.0)
    high, low = halves(panel[...])
    panel_high[...] = high
    panel_low[...] = low
    out = thrice((reflect_high[...], reflect_low[...]), (panel_high[...], panel_low[...]))
    own = pl.ds(pl.multiple_of(where_ref[1] * SIDE, SIDE), SIDE)
    mine_high, mine_low = panel_high[own, :], panel_low[own, :]
    out_high, out_low = halves(out)
    for position, ref in enumerate(out_refs):
        side = pl.ds(0, SIDE) if position < 2 else pl.ds(SIDE, SIDE)
        top, bottom = (out_high, mine_high) if position % 2 == 0 else (out_low, mine_low)
        cut = slice(0, SIDE) if position < 2 else slice(SIDE, 2 * SIDE)
        ref[0, 0:SIDE, :] = top[:, cut]
        ref[0, SIDE:2 * SIDE, :] = bottom[:, cut]


def joint_of(where, reflect, packed):
    count, kept, _ = packed.shape
    block, order = reflect.shape
    steps = count // 2
    low_half = pl.BlockSpec((1, 2 * SIDE, SIDE), lambda n: (n, 0, 0))
    high_half = pl.BlockSpec((1, 2 * SIDE, SIDE), lambda n: (steps - 1 - n, 0, 0))
    return pl.pallas_call(
        joint_kernel,
        grid=(steps,),
        in_specs=[
            smem,
            pl.BlockSpec((block, order), lambda n: (0, 0)),
            pl.BlockSpec((1, kept, SIDE), lambda n: (n, 0, 0)),
            pl.BlockSpec((1, kept, SIDE), lambda n: (count - 1 - n, 0, 0)),
        ],
        out_specs=[low_half, low_half, high_half, high_half],
        out_shape=[shaped(steps, 2 * SIDE, SIDE, dtype=jnp.bfloat16)] * 4,
        scratch_shapes=[pltpu.VMEM((block, order), jnp.bfloat16)] * 2
        + [pltpu.VMEM((order, 2 * SIDE), jnp.bfloat16)] * 2
        + [pltpu.VMEM((order, 2 * SIDE), jnp.float32)],
        compiler_params=params(),
        cost_estimate=pl.CostEstimate(
            flops=6 * block * order * order, bytes_accessed=4 * packed.size, transcendentals=0
        ),
        name="joint",
    )(where, reflect, packed, packed)


def level_kernel(where_ref, upper_ref, lower_ref, *refs):
    joint_refs, (keep_ref, give_ref) = refs[:4], refs[4:]
    steps = keep_ref.shape[0]
    first = where_ref[0] == 0
    left = halves(jnp.concatenate([upper_ref[...], lower_ref[...]], axis=1))
    for n in range(steps):
        at = 2 * n
        high_ref, low_ref = joint_refs[:2] if at < steps else joint_refs[2:]
        at = at % steps
        high = jnp.concatenate([high_ref[at], high_ref[at + 1]], axis=1)
        low = jnp.concatenate([low_ref[at], low_ref[at + 1]], axis=1)
        out = thrice(left, (high, low))
        even, odd = out[:, :SIDE], out[:, SIDE:]
        keep_ref[n] = jnp.where(first, even, odd)
        give_ref[n] = jnp.where(first, odd, even)


def level_of(where, upper, lower, joint):
    columns = upper.shape[0]
    steps = joint[0].shape[0]
    return pl.pallas_call(
        level_kernel,
        in_specs=[smem] + [pl.BlockSpec(memory_space=pltpu.VMEM)] * 6,
        out_shape=[shaped(steps, columns, SIDE)] * 2,
        compiler_params=params(),
        name="level",
    )(where, upper, lower, *joint)


def inverse_kernel(packed_ref, out_ref):
    count = packed_ref.shape[0]
    for q in range(count // 2):
        a, b = 2 * q, 2 * q + 1
        left, right = packed_ref[a, 0], packed_ref[b, 0]
        cross = full(full(left, packed_ref[a, 1]), right)
        out_ref[q, 0:SIDE, 0:SIDE] = left
        out_ref[q, 0:SIDE, SIDE:2 * SIDE] = -cross
        out_ref[q, SIDE:2 * SIDE, 0:SIDE] = jnp.zeros((SIDE, SIDE), jnp.float32)
        out_ref[q, SIDE:2 * SIDE, SIDE:2 * SIDE] = right


def inverse_of(packed):
    count = packed.shape[0]
    return pl.pallas_call(
        inverse_kernel,
        grid=(1,),
        in_specs=[pl.BlockSpec((count, 2, SIDE, SIDE), lambda n: (0, 0, 0, 0))],
        out_specs=pl.BlockSpec((count // 2, 2 * SIDE, 2 * SIDE), lambda n: (0, 0, 0)),
        out_shape=shaped(count // 2, 2 * SIDE, 2 * SIDE),
        compiler_params=params(),
        name="inverse",
    )(packed)


def band_block(packed_ref, row, column):
    kept = packed_ref.shape[1]
    count = packed_ref.shape[0]
    if column - row < kept:
        return packed_ref[row, column - row]
    return packed_ref[count - 1 - row, column - count // 2]


def final_kernel(
    where_ref, own_ref, other_ref, summit_ref, lower_ref, reflect_ref, packed_ref, inverse_ref,
    out_ref, solved_ref, whole_ref,
):
    parity = where_ref[0]
    count = packed_ref.shape[0]
    steps = own_ref.shape[0]
    for n in range(steps):
        even, odd = pick(parity, own_ref[n], other_ref[n])
        whole_ref[2 * n * SIDE:(2 * n + 1) * SIDE, :] = even
        whole_ref[(2 * n + 1) * SIDE:(2 * n + 2) * SIDE, :] = odd
    out_ref[...] = summit_ref[...] - thrice(halves(reflect_ref[...]), halves(whole_ref[...]))
    whole_ref[...] = lower_ref[...] - whole_ref[...]
    for q in reversed(range(count // 2)):
        rows = pl.ds(2 * q * SIDE, 2 * SIDE)
        value = whole_ref[rows, :]
        if q < count // 2 - 1:
            band = jnp.concatenate(
                [
                    jnp.concatenate(
                        [band_block(packed_ref, k, j) for j in range(2 * q + 2, count)], axis=1
                    )
                    for k in (2 * q, 2 * q + 1)
                ],
                axis=0,
            )
            value = value - full(band, whole_ref[(2 * q + 2) * SIDE:, :])
        whole_ref[rows, :] = full(inverse_ref[q], value)
    mine = pl.ds(pl.multiple_of(where_ref[1] * SIDE, SIDE), SIDE)
    solved_ref[...] = whole_ref[mine, :].T


def final_of(where, own, other, summit, lower, reflect, packed, inverse):
    columns = summit.shape[1]
    return pl.pallas_call(
        final_kernel,
        in_specs=[smem] + [pl.BlockSpec(memory_space=pltpu.VMEM)] * 7,
        out_shape=[shaped(SIDE, columns), shaped(columns, SIDE)],
        scratch_shapes=[pltpu.VMEM(lower.shape, jnp.float32)],
        compiler_params=params(),
        name="final",
    )(where, own, other, summit, lower, reflect, packed, inverse)


def moved(value, axis, pairs):
    return lax.ppermute(value, axis, pairs)


def per_device(
    right_side, reflectors, leaf_factor, node_reflect, node_factor, upper_blocks, block_inverse
):
    block = upper_blocks.shape[0]
    columns = right_side.shape[1]
    count = lax.axis_size("leaf")
    rows = lax.axis_size("rows")
    half = count // 2
    kept = half + 1
    row_index = lax.axis_index("rows")
    leaf_index = lax.axis_index("leaf")
    where = jnp.stack([leaf_index % 2, leaf_index]).astype(jnp.int32)
    swap = [(i, i ^ 1) for i in range(count)]
    same = [list(range(k, count, 2)) for k in range(2)]

    def scatter_sum(parts):
        keep, give = parts
        pair = keep + moved(give, "leaf", swap)
        got = lax.all_to_all(pair, "leaf", 0, 0, axis_index_groups=same)
        return jnp.sum(got, axis=0)

    def copies(mine):
        return jnp.broadcast_to(mine[None], (half,) + mine.shape)

    def collect(spread):
        own = lax.all_to_all(spread, "leaf", 0, 0, axis_index_groups=same)
        return own, moved(own, "leaf", swap)

    def packed_whole(blocks, pairs, shift):
        given = moved(blocks[kept:], "leaf", pairs)
        padded = jnp.pad(given, ((kept, 2), (0, 0), (0, 0)))
        placed = lax.dynamic_slice_in_dim(padded, jnp.maximum(kept - shift, 0), kept, 0)
        return lax.all_gather(blocks[:kept] + placed, "leaf", axis=0)

    factor_blocks = node_factor[0].reshape(count, block, block)
    factor_packed = packed_whole(
        factor_blocks, [(d, count - 1 - d) for d in range(half, count)], leaf_index + 1
    )
    upper_list = upper_blocks.reshape(block, count, block).transpose(1, 0, 2)
    upper_list = lax.dynamic_slice_in_dim(
        jnp.pad(upper_list, ((0, count), (0, 0), (0, 0))), leaf_index, count, 0
    )
    upper_list = jnp.concatenate([block_inverse[None], upper_list[1:]], axis=0)
    upper_packed = packed_whole(
        upper_list, [(d, count - 1 - d) for d in range(half)], count - leaf_index
    )

    weights = collect(copies(scatter_sum(weights_of(where, right_side, reflectors))))
    coeffs = collect(coeffs_of(where, *weights, leaf_factor[0]))
    rotated, top = lowered_of(where, *coeffs, reflectors, right_side)

    joint = joint_of(where, node_reflect[0], factor_packed.reshape(count, kept * block, block))

    stride = 1
    upper = top
    lower = moved(top, "rows", [(i, i + 1) for i in range(0, rows, 2)])
    own_coeffs = jnp.zeros_like(top)
    own_top = top
    while stride < rows:
        if stride > 1:
            nodes = list(range(stride, rows, 2 * stride))
            upper = moved(lower, "rows", [(j + stride // 2, j) for j in nodes])
            lower = moved(lower, "rows", [(j - stride // 2, j) for j in nodes])
        if 2 * stride == rows:
            lower_whole = lax.all_gather(lower.T, "leaf", axis=0, tiled=True)
        share = scatter_sum(level_of(where, upper, lower, joint))
        lower = lower - share
        mine = row_index % (2 * stride) == stride
        own_coeffs = jnp.where(mine, share, own_coeffs)
        own_top = jnp.where(mine, upper, own_top)
        stride *= 2
    root = rows // 2

    back = moved(lower, "rows", [(root, 0)])
    own, other = collect(copies(own_coeffs.T))
    inverse = inverse_of(upper_packed)
    lowered, solved = final_of(
        where, own, other, own_top.T, lower_whole, node_reflect[0], upper_packed, inverse
    )
    final_top = jnp.where(row_index == 0, back.T, lowered)
    rotated = lax.dynamic_update_slice_in_dim(rotated, final_top, 0, 0)
    arrived = lax.all_to_all(solved.reshape(rows, columns // rows, block), "rows", 0, 0)[root]
    return (rotated, arrived.T)


def solution(mesh):
    in_specs = (
        P(("rows", "leaf"), None),
        P(("rows", "leaf"), None),
        P("rows", None, "leaf"),
        P("rows", "leaf", None),
        P("rows", None, "leaf"),
        P("leaf", None),
        P("leaf", None),
    )
    out_specs = (P(("rows", "leaf"), None), P("leaf", "rows"))
    return jax.shard_map(
        per_device, mesh=mesh, in_specs=in_specs, out_specs=out_specs, check_vma=False
    )
```

```python
import functools

import jax
import jax.numpy as jnp
from jax import lax
from jax.experimental import pallas as pl
from jax.experimental.pallas import tpu as pltpu
from jax.sharding import PartitionSpec as P

SIDE = 128
GROUP = 2
SPLIT = (((1,), (0,)), ((), ()))
LIMIT = 28 * 1024 * 1024


def halves(value):
    high = value.astype(jnp.bfloat16)
    low = (value - high.astype(jnp.float32)).astype(jnp.bfloat16)
    return high, low


def once(left, right):
    return lax.dot_general(left, right, SPLIT, preferred_element_type=jnp.float32)


def thrice(left, right):
    return once(left[0], right[0]) + (once(left[0], right[1]) + once(left[1], right[0]))


def full(left, right):
    return lax.dot_general(
        left, right, SPLIT, precision=lax.Precision.HIGHEST, preferred_element_type=jnp.float32
    )


def pick(parity, own, other):
    first = parity == 0
    return jnp.where(first, own, other), jnp.where(first, other, own)


smem = pl.BlockSpec(memory_space=pltpu.SMEM)


vmem = pl.BlockSpec(memory_space=pltpu.VMEM)


def params():
    return pltpu.CompilerParams(vmem_limit_bytes=LIMIT)


def cost(flops, size):
    return pl.CostEstimate(flops=flops, bytes_accessed=size, transcendentals=0)


def shaped(*shape, dtype=jnp.float32):
    return jax.ShapeDtypeStruct(shape, dtype)


def weights_kernel(where_ref, side_ref, vectors_ref, keep_ref, give_ref, high_ref, low_ref):
    @pl.when(pl.program_id(0) == 0)
    def _():
        high, low = halves(side_ref[...].T)
        high_ref[...] = high
        low_ref[...] = low

    first = where_ref[0] == 0
    for n in range(keep_ref.shape[0]):
        vectors = vectors_ref[:, 2 * n * SIDE:(2 * n + 2) * SIDE]
        out = thrice((high_ref[...], low_ref[...]), halves(vectors))
        even, odd = out[:, :SIDE], out[:, SIDE:]
        keep_ref[n] = jnp.where(first, even, odd)
        give_ref[n] = jnp.where(first, odd, even)


def weights_of(where, side, vectors):
    tall, order = vectors.shape
    columns = side.shape[1]
    steps = order // (2 * SIDE)
    block = pl.BlockSpec((GROUP, columns, SIDE), lambda n: (n, 0, 0))
    return pl.pallas_call(
        weights_kernel,
        grid=(steps // GROUP,),
        in_specs=[
            smem,
            pl.BlockSpec((tall, columns), lambda n: (0, 0)),
            pl.BlockSpec((tall, 2 * GROUP * SIDE), lambda n: (0, n)),
        ],
        out_specs=[block, block],
        out_shape=[shaped(steps, columns, SIDE)] * 2,
        scratch_shapes=[pltpu.VMEM((columns, tall), jnp.bfloat16)] * 2,
        compiler_params=params(),
        cost_estimate=cost(6 * tall * columns * order, 4 * vectors.size),
        name="weights",
    )(where, side, vectors)


def coeffs_kernel(where_ref, own_ref, other_ref, factor_ref, out_ref):
    parity = where_ref[0]
    steps = own_ref.shape[0]
    total = jnp.zeros(own_ref.shape[1:], jnp.float32)
    for n in range(steps):
        left = jnp.concatenate(pick(parity, own_ref[n], other_ref[n]), axis=1)
        right = factor_ref[2 * n * SIDE:(2 * n + 2) * SIDE, :]
        total = total + thrice(halves(left), halves(right))
    total = total.T
    for n in range(steps):
        out_ref[n] = total


def coeffs_of(where, own, other, factor):
    return pl.pallas_call(
        coeffs_kernel,
        in_specs=[smem] + [pl.BlockSpec(memory_space=pltpu.VMEM)] * 3,
        out_shape=shaped(own.shape[0], SIDE, own.shape[1]),
        compiler_params=params(),
        cost_estimate=cost(6 * own.shape[1] * factor.size, 4 * factor.size),
        name="coeffs",
    )(where, own, other, factor)


def lowered_kernel(where_ref, own_ref, other_ref, vectors_ref, side_ref, out_ref, top_ref):
    step = pl.program_id(0)

    @pl.when(step == 0)
    def _():
        out_ref[...] = side_ref[...]

    total = out_ref[...]
    for n in range(own_ref.shape[0]):
        right = jnp.concatenate(pick(where_ref[0], own_ref[n], other_ref[n]), axis=0)
        vectors = vectors_ref[:, 2 * n * SIDE:(2 * n + 2) * SIDE]
        total = total - thrice(halves(vectors), halves(right))
    out_ref[...] = total

    @pl.when(step == pl.num_programs(0) - 1)
    def _():
        top_ref[...] = out_ref[:SIDE, :].T


def lowered_of(where, own, other, vectors, side):
    tall, order = vectors.shape
    columns = side.shape[1]
    steps = order // (2 * SIDE)
    block = pl.BlockSpec((GROUP, SIDE, columns), lambda n: (n, 0, 0))
    whole = pl.BlockSpec((tall, columns), lambda n: (0, 0))
    return pl.pallas_call(
        lowered_kernel,
        grid=(steps // GROUP,),
        in_specs=[
            smem, block, block, pl.BlockSpec((tall, 2 * GROUP * SIDE), lambda n: (0, n)), whole,
        ],
        out_specs=[whole, pl.BlockSpec((columns, SIDE), lambda n: (0, 0))],
        out_shape=[shaped(tall, columns), shaped(columns, SIDE)],
        compiler_params=params(),
        cost_estimate=cost(6 * tall * columns * order, 4 * vectors.size),
        name="lowered",
    )(where, own, other, vectors, side)


def joint_kernel(where_ref, reflect_ref, packed_ref, high_ref, low_ref, panel_ref, sems):
    count, kept, _ = packed_ref.shape
    order = reflect_ref.shape[1]
    steps = count // 2
    copies = []
    for n in range(steps):
        pair = []
        for k in (n, count - 1 - n):
            copy = pltpu.make_async_copy(packed_ref.at[k], panel_ref.at[k], sems.at[k])
            copy.start()
            pair.append(copy)
        copies.append(pair)
    reflect = halves(reflect_ref[...])
    own = where_ref[1]
    spare = kept // SIDE - 1
    for n in range(steps):
        for copy in copies[n]:
            copy.wait()
        far = count - 1 - n
        edge = (n + 1) * SIDE
        stop = order - n * SIDE
        short, long = halves(panel_ref[n]), halves(panel_ref[far])
        shared = [jnp.concatenate([s[:edge], t[:edge]], axis=1) for s, t in zip(short, long)]
        rest = [
            jnp.concatenate([t[edge:], s[edge:kept - SIDE]], axis=0)
            if stop > kept else t[edge:stop]
            for s, t in zip(short, long)
        ]
        both = thrice([r[:, :edge] for r in reflect], shared)
        left = both[:, :SIDE]
        right = both[:, SIDE:] + thrice([r[:, edge:stop] for r in reflect], rest)

        def rows(k, at):
            return panel_ref[k, pl.ds(pl.multiple_of(at * SIDE, SIDE), SIDE), :]

        zero = jnp.zeros((SIDE, SIDE), jnp.float32)
        own_left = jnp.where(own <= n, rows(n, jnp.minimum(own, spare)), zero)
        moved_on = jnp.clip(own + n - spare, 0, spare)
        own_right = jnp.where(
            own <= spare,
            rows(far, jnp.minimum(own, spare)),
            jnp.where(own <= far, rows(n, moved_on), zero),
        )
        for k, top, bottom in ((n, left, own_left), (far, right, own_right)):
            at = pl.ds(k * SIDE, SIDE)
            for ref, part in zip((high_ref, low_ref), zip(halves(top), halves(bottom))):
                ref[0:SIDE, at] = part[0]
                ref[SIDE:2 * SIDE, at] = part[1]


def joint_of(where, reflect, packed):
    block, order = reflect.shape
    return pl.pallas_call(
        joint_kernel,
        in_specs=[smem, vmem, pl.BlockSpec(memory_space=pl.ANY)],
        out_specs=[vmem] * 2,
        out_shape=[shaped(2 * block, order, dtype=jnp.bfloat16)] * 2,
        scratch_shapes=[
            pltpu.VMEM(packed.shape, jnp.float32),
            pltpu.SemaphoreType.DMA((packed.shape[0],)),
        ],
        compiler_params=params(),
        cost_estimate=cost(3 * block * order * order, 4 * packed.size),
        name="joint",
    )(where, reflect, packed)


def level_kernel(where_ref, upper_ref, lower_ref, high_ref, low_ref, keep_ref, give_ref):
    first = where_ref[0] == 0
    left = halves(jnp.concatenate([upper_ref[...], lower_ref[...]], axis=1))
    for n in range(keep_ref.shape[0]):
        at = pl.ds(2 * n * SIDE, 2 * SIDE)
        out = thrice(left, (high_ref[:, at], low_ref[:, at]))
        even, odd = out[:, :SIDE], out[:, SIDE:]
        keep_ref[n] = jnp.where(first, even, odd)
        give_ref[n] = jnp.where(first, odd, even)


def level_of(where, upper, lower, joint):
    columns = upper.shape[0]
    wide, order = joint[0].shape
    steps = order // (2 * SIDE)
    return pl.pallas_call(
        level_kernel,
        in_specs=[smem] + [vmem] * 4,
        out_specs=[vmem] * 2,
        out_shape=[shaped(steps, columns, SIDE)] * 2,
        compiler_params=params(),
        cost_estimate=cost(6 * columns * wide * order, 4 * wide * order),
        name="level",
    )(where, upper, lower, *joint)


def fold_kernel(pieces_ref, out_ref):
    count = pieces_ref.shape[0]
    for n in range(count // 2):
        far = count - 1 - n
        out_ref[n, 0:far] = pieces_ref[n, n + 1:count]
        out_ref[n, far] = pieces_ref[n, count]
        for k in range(far + 1, count):
            out_ref[n, k] = pieces_ref[far, k]
        out_ref[n, count] = pieces_ref[far, count]


def fold_of(pieces):
    count = pieces.shape[0]
    return pl.pallas_call(
        fold_kernel,
        in_specs=[vmem],
        out_specs=vmem,
        out_shape=shaped(count // 2, *pieces.shape[1:]),
        compiler_params=params(),
        name="fold",
    )(pieces)


def final_kernel(
    where_ref, own_ref, other_ref, summit_ref, reflect_ref, folded_ref,
    out_ref, solved_ref, coeffs_ref, whole_ref, panel_ref, sems,
):
    parity = where_ref[0]
    steps = own_ref.shape[0]
    count = 2 * steps
    copies = []
    for p in range(count // 4):
        copy = pltpu.make_async_copy(
            folded_ref.at[:, 2 * p:2 * p + 2], panel_ref.at[p], sems.at[p]
        )
        copy.start()
        copies.append(copy)
    for n in range(steps):
        for part, ref in enumerate((coeffs_ref, whole_ref)):
            even, odd = pick(parity, own_ref[n, part], other_ref[n, part])
            ref[2 * n * SIDE:(2 * n + 1) * SIDE, :] = even
            ref[(2 * n + 1) * SIDE:(2 * n + 2) * SIDE, :] = odd
    out_ref[...] = summit_ref[...] - thrice(halves(reflect_ref[...]), halves(coeffs_ref[...]))

    def block_at(row, column):
        near = min(row, count - 1 - row)
        if row >= count // 2:
            at = column
        else:
            at = count - 1 - row if column == count else column - row - 1
        return panel_ref[near // 2, :, near % 2, at].reshape(SIDE, SIDE)

    zero = jnp.zeros((SIDE, SIDE), jnp.float32)
    for q in reversed(range(count // 2)):
        if q >= count // 4:
            copies[count // 2 - 1 - q].wait()
        a, b = 2 * q, 2 * q + 1
        rows = pl.ds(a * SIDE, 2 * SIDE)
        value = whole_ref[rows, :]
        if b < count - 1:
            band = jnp.concatenate(
                [
                    jnp.concatenate([block_at(k, j) for j in range(b + 1, count)], axis=1)
                    for k in (a, b)
                ],
                axis=0,
            )
            value = value - full(band, whole_ref[(b + 1) * SIDE:, :])
        inverse = jnp.concatenate(
            [
                jnp.concatenate([block_at(a, count), -block_at(a, b)], axis=1),
                jnp.concatenate([zero, block_at(b, count)], axis=1),
            ],
            axis=0,
        )
        whole_ref[rows, :] = full(inverse, value)
    mine = pl.ds(pl.multiple_of(where_ref[1] * SIDE, SIDE), SIDE)
    solved_ref[...] = whole_ref[mine, :].T


def final_of(where, own, other, summit, reflect, folded):
    columns = summit.shape[1]
    order = reflect.shape[1]
    rows, near, long = folded.shape[:3]
    return pl.pallas_call(
        final_kernel,
        in_specs=[smem] + [vmem] * 4 + [pl.BlockSpec(memory_space=pl.ANY)],
        out_specs=[vmem] * 2,
        out_shape=[shaped(SIDE, columns), shaped(columns, SIDE)],
        scratch_shapes=[pltpu.VMEM((order, columns), jnp.float32)] * 2
        + [
            pltpu.VMEM((near // 2, rows, 2, long) + folded.shape[3:], jnp.float32),
            pltpu.SemaphoreType.DMA((near // 2,)),
        ],
        compiler_params=params(),
        cost_estimate=cost(8 * columns * order * order, 4 * folded.size),
        name="final",
    )(where, own, other, summit, reflect, folded)


def dot(left, right):
    return jnp.dot(left, right, precision=lax.Precision.HIGHEST, preferred_element_type=jnp.float32)


def moved(value, axis, pairs):
    return lax.ppermute(value, axis, pairs)


def per_device(
    right_side, reflectors, leaf_factor, node_reflect, node_factor, upper_blocks, block_inverse
):
    block = upper_blocks.shape[0]
    columns = right_side.shape[1]
    count = lax.axis_size("leaf")
    rows = lax.axis_size("rows")
    half = count // 2
    kept = half + 1
    row_index = lax.axis_index("rows")
    leaf_index = lax.axis_index("leaf")
    where = jnp.stack([leaf_index % 2, leaf_index]).astype(jnp.int32)
    swap = [(i, i ^ 1) for i in range(count)]
    same = [list(range(k, count, 2)) for k in range(2)]

    def scatter_sum(parts):
        keep, give = parts
        pair = keep + moved(give, "leaf", swap)
        got = lax.all_to_all(pair, "leaf", 0, 0, axis_index_groups=same)
        return jnp.sum(got, axis=0)

    def copies(mine):
        return jnp.broadcast_to(mine[None], (half,) + mine.shape)

    def collect(spread):
        own = lax.all_to_all(spread, "leaf", 0, 0, axis_index_groups=same)
        return own, moved(own, "leaf", swap)

    factor_blocks = node_factor[0].reshape(count, block, block)
    given = moved(
        factor_blocks[kept:], "leaf", [(d, count - 1 - d) for d in range(half, count)]
    )
    weights_part = scatter_sum(weights_of(where, right_side, reflectors))

    given, _ = lax.optimization_barrier((given, weights_part))
    padded = jnp.pad(given, ((kept, 2), (0, 0), (0, 0)))
    placed = lax.dynamic_slice_in_dim(padded, jnp.maximum(half - leaf_index, 0), kept, 0)
    factor_packed = lax.all_gather(factor_blocks[:kept] + placed, "leaf", axis=0)

    weights = collect(copies(weights_part))
    coeffs = collect(coeffs_of(where, *weights, leaf_factor[0]))
    rotated, top = lowered_of(where, *coeffs, reflectors, right_side)

    upper_own, inverse_own, _ = lax.optimization_barrier((upper_blocks, block_inverse, top))
    inverse_next = moved(inverse_own, "leaf", [(i + 1, i) for i in range(0, count, 2)])
    eighth = block // rows
    upper_slice = lax.dynamic_slice_in_dim(upper_own, row_index * eighth, eighth, 0)
    inverse_slice = lax.dynamic_slice_in_dim(inverse_own, row_index * eighth, eighth, 0)
    upper_slice = upper_slice.reshape(eighth, count, block).transpose(1, 0, 2)
    beside = lax.dynamic_slice_in_dim(
        upper_own, jnp.minimum(leaf_index + 1, count - 1) * block, block, 1
    )
    cross = dot(dot(inverse_slice, beside), inverse_next)
    at_cross = jnp.arange(count)[:, None, None] == leaf_index + 1
    at_cross = jnp.logical_and(at_cross, leaf_index % 2 == 0)
    upper_slice = jnp.where(at_cross, cross[None], upper_slice)
    upper_slice = jnp.concatenate([upper_slice, inverse_slice[None]], axis=0)
    folded = fold_of(lax.all_gather(upper_slice, "leaf", axis=0))
    folded = lax.all_gather(folded, "rows", axis=0)

    joint = joint_of(where, node_reflect[0], factor_packed.reshape(count, kept * block, block))

    stride = 1
    upper = top
    lower = moved(top, "rows", [(i, i + 1) for i in range(0, rows, 2)])
    own_coeffs = jnp.zeros_like(top)
    own_top = top
    while stride < rows:
        if stride > 1:
            nodes = list(range(stride, rows, 2 * stride))
            upper = moved(lower, "rows", [(j + stride // 2, j) for j in nodes])
            lower = moved(lower, "rows", [(j - stride // 2, j) for j in nodes])
        share = scatter_sum(level_of(where, upper, lower, joint))
        lower = lower - share
        mine = row_index % (2 * stride) == stride
        own_coeffs = jnp.where(mine, share, own_coeffs)
        own_top = jnp.where(mine, upper, own_top)
        stride *= 2
    root = rows // 2

    back = moved(lower, "rows", [(root, 0)])
    own, other = collect(copies(jnp.stack([own_coeffs.T, lower.T])))
    lowered, solved = final_of(where, own, other, own_top.T, node_reflect[0], folded)
    final_top = jnp.where(row_index == 0, back.T, lowered)
    rotated = lax.dynamic_update_slice_in_dim(rotated, final_top, 0, 0)
    arrived = lax.all_to_all(solved.reshape(rows, columns // rows, block), "rows", 0, 0)[root]
    return (rotated, arrived.T)


def solution(mesh):
    in_specs = (
        P(("rows", "leaf"), None),
        P(("rows", "leaf"), None),
        P("rows", None, "leaf"),
        P("rows", "leaf", None),
        P("rows", None, "leaf"),
        P("leaf", None),
        P("leaf", None),
    )
    out_specs = (P(("rows", "leaf"), None), P("leaf", "rows"))
    return jax.shard_map(
        per_device, mesh=mesh, in_specs=in_specs, out_specs=out_specs, check_vma=False
    )
```

```python
import functools

import jax
import jax.numpy as jnp
from jax import lax
from jax.experimental import pallas as pl
from jax.experimental.pallas import tpu as pltpu
from jax.sharding import PartitionSpec as P

SIDE = 128
GROUP = 4
SPLIT = (((1,), (0,)), ((), ()))
SMALL = 24 * 1024 * 1024
LARGE = 56 * 1024 * 1024


def halves(value):
    high = value.astype(jnp.bfloat16)
    low = (value - high.astype(jnp.float32)).astype(jnp.bfloat16)
    return high, low


def once(left, right):
    return lax.dot_general(left, right, SPLIT, preferred_element_type=jnp.float32)


def thrice(left, right):
    return once(left[0], right[0]) + (once(left[0], right[1]) + once(left[1], right[0]))


def stacked(left, right):
    size = left[0].shape[0]
    both = once(jnp.concatenate(left, axis=0), right[0])
    return both[:size] + (both[size:] + once(left[0], right[1]))


def pick(parity, own, other):
    first = parity == 0
    return jnp.where(first, own, other), jnp.where(first, other, own)


smem = pl.BlockSpec(memory_space=pltpu.SMEM)


vmem = pl.BlockSpec(memory_space=pltpu.VMEM)


def params(limit=SMALL):
    return pltpu.CompilerParams(vmem_limit_bytes=limit)


def cost(flops, size):
    return pl.CostEstimate(flops=flops, bytes_accessed=size, transcendentals=0)


def shaped(*shape, dtype=jnp.float32):
    return jax.ShapeDtypeStruct(shape, dtype)


def weights_kernel(where_ref, side_ref, vectors_ref, keep_ref, give_ref, high_ref, low_ref):
    @pl.when(pl.program_id(0) == 0)
    def _():
        high, low = halves(side_ref[...].T)
        high_ref[...] = high
        low_ref[...] = low

    first = where_ref[0] == 0
    for n in range(keep_ref.shape[0]):
        vectors = vectors_ref[:, 2 * n * SIDE:(2 * n + 2) * SIDE]
        out = stacked((high_ref[...], low_ref[...]), halves(vectors))
        even, odd = out[:, :SIDE], out[:, SIDE:]
        keep_ref[n] = jnp.where(first, even, odd)
        give_ref[n] = jnp.where(first, odd, even)


def weights_of(where, side, vectors):
    tall, order = vectors.shape
    columns = side.shape[1]
    steps = order // (2 * SIDE)
    block = pl.BlockSpec((GROUP, columns, SIDE), lambda n: (n, 0, 0))
    return pl.pallas_call(
        weights_kernel,
        grid=(steps // GROUP,),
        in_specs=[
            smem,
            pl.BlockSpec((tall, columns), lambda n: (0, 0)),
            pl.BlockSpec((tall, 2 * GROUP * SIDE), lambda n: (0, n)),
        ],
        out_specs=[block, block],
        out_shape=[shaped(steps, columns, SIDE)] * 2,
        scratch_shapes=[pltpu.VMEM((columns, tall), jnp.bfloat16)] * 2,
        compiler_params=params(LARGE),
        cost_estimate=cost(6 * tall * columns * order, 4 * vectors.size),
        name="weights",
    )(where, side, vectors)


def coeffs_kernel(where_ref, own_ref, other_ref, factor_ref, out_ref):
    parity = where_ref[0]
    steps = own_ref.shape[0]
    total = jnp.zeros(own_ref.shape[1:], jnp.float32)
    for n in range(steps):
        left = jnp.concatenate(pick(parity, own_ref[n], other_ref[n]), axis=1)
        right = factor_ref[2 * n * SIDE:(2 * n + 2) * SIDE, :]
        total = total + stacked(halves(left), halves(right))
    total = total.T
    for n in range(steps):
        out_ref[n] = total


def coeffs_of(where, own, other, factor):
    return pl.pallas_call(
        coeffs_kernel,
        in_specs=[smem] + [pl.BlockSpec(memory_space=pltpu.VMEM)] * 3,
        out_shape=shaped(own.shape[0], SIDE, own.shape[1]),
        compiler_params=params(),
        cost_estimate=cost(6 * own.shape[1] * factor.size, 4 * factor.size),
        name="coeffs",
    )(where, own, other, factor)


def lowered_kernel(where_ref, own_ref, other_ref, vectors_ref, side_ref, out_ref, top_ref):
    step = pl.program_id(0)

    @pl.when(step == 0)
    def _():
        out_ref[...] = side_ref[...]

    total = out_ref[...]
    for n in range(own_ref.shape[0]):
        right = jnp.concatenate(pick(where_ref[0], own_ref[n], other_ref[n]), axis=0)
        vectors = vectors_ref[:, 2 * n * SIDE:(2 * n + 2) * SIDE]
        total = total - thrice(halves(vectors), halves(right))
    out_ref[...] = total

    @pl.when(step == pl.num_programs(0) - 1)
    def _():
        top_ref[...] = out_ref[:SIDE, :].T


def lowered_of(where, own, other, vectors, side):
    tall, order = vectors.shape
    columns = side.shape[1]
    steps = order // (2 * SIDE)
    block = pl.BlockSpec((GROUP, SIDE, columns), lambda n: (n, 0, 0))
    whole = pl.BlockSpec((tall, columns), lambda n: (0, 0))
    return pl.pallas_call(
        lowered_kernel,
        grid=(steps // GROUP,),
        in_specs=[
            smem, block, block, pl.BlockSpec((tall, 2 * GROUP * SIDE), lambda n: (0, n)), whole,
        ],
        out_specs=[whole, pl.BlockSpec((columns, SIDE), lambda n: (0, 0))],
        out_shape=[shaped(tall, columns), shaped(columns, SIDE)],
        compiler_params=params(LARGE),
        cost_estimate=cost(6 * tall * columns * order, 4 * vectors.size),
        name="lowered",
    )(where, own, other, vectors, side)


def slot_of(k, count):
    return (k + 10) % count if k < count - 2 else k + 2 - count


def joint_kernel(where_ref, reflect_ref, factor_ref, high_ref, low_ref, panel_ref, sems):
    count, kept, _ = factor_ref.shape
    order = reflect_ref.shape[1]
    steps = count // 2
    spare = order - kept
    copies = [None] * count
    for n in range(steps):
        for k in (n, n + steps):
            edge = (k + 1) * SIDE
            rows = pl.ds(0, min(edge, kept))
            copies[k] = [
                pltpu.make_async_copy(factor_ref.at[k, rows], panel_ref.at[k, rows], sems.at[0, k])
            ]
            if edge > kept:
                copies[k].append(
                    pltpu.make_async_copy(
                        factor_ref.at[slot_of(k, count), pl.ds(kept - spare, edge - kept)],
                        panel_ref.at[k, pl.ds(kept, edge - kept)],
                        sems.at[1, k],
                    )
                )
            for copy in copies[k]:
                copy.start()
    reflect = halves(reflect_ref[...])
    own = where_ref[1]
    zero = jnp.zeros((SIDE, SIDE), jnp.float32)
    for n in range(steps):
        far = n + steps
        for copy in copies[n] + copies[far]:
            copy.wait()
        edge, stop = (n + 1) * SIDE, (far + 1) * SIDE
        near_part, far_part = halves(panel_ref[n, 0:edge]), halves(panel_ref[far, 0:stop])
        shared = [jnp.concatenate([s, t[:edge]], axis=1) for s, t in zip(near_part, far_part)]
        both = stacked([r[:, :edge] for r in reflect], shared)
        rest = stacked([r[:, edge:stop] for r in reflect], [t[edge:] for t in far_part])
        for k, top in ((n, both[:, :SIDE]), (far, both[:, SIDE:] + rest)):
            mine = pl.ds(pl.multiple_of(jnp.minimum(own, k) * SIDE, SIDE), SIDE)
            bottom = jnp.where(own <= k, panel_ref[k, mine, :], zero)
            at = pl.ds(k * SIDE, SIDE)
            for ref, part in zip((high_ref, low_ref), zip(halves(top), halves(bottom))):
                ref[0:SIDE, at] = part[0]
                ref[SIDE:2 * SIDE, at] = part[1]


def joint_of(where, reflect, factor):
    block, order = reflect.shape
    count = factor.shape[0]
    return pl.pallas_call(
        joint_kernel,
        in_specs=[smem, vmem, pl.BlockSpec(memory_space=pltpu.HBM)],
        out_specs=[vmem] * 2,
        out_shape=[shaped(2 * block, order, dtype=jnp.bfloat16)] * 2,
        scratch_shapes=[
            pltpu.VMEM((count, order, SIDE), jnp.float32),
            pltpu.SemaphoreType.DMA((2, count)),
        ],
        compiler_params=params(LARGE),
        cost_estimate=cost(3 * block * order * order, 2 * factor.size),
        name="joint",
    )(where, reflect, factor)


def level_kernel(where_ref, upper_ref, lower_ref, high_ref, low_ref, keep_ref, give_ref):
    first = where_ref[0] == 0
    left = halves(jnp.concatenate([upper_ref[...], lower_ref[...]], axis=1))
    for n in range(keep_ref.shape[0]):
        at = pl.ds(2 * n * SIDE, 2 * SIDE)
        out = stacked(left, (high_ref[:, at], low_ref[:, at]))
        even, odd = out[:, :SIDE], out[:, SIDE:]
        keep_ref[n] = jnp.where(first, even, odd)
        give_ref[n] = jnp.where(first, odd, even)


def level_of(where, upper, lower, joint):
    columns = upper.shape[0]
    wide, order = joint[0].shape
    steps = order // (2 * SIDE)
    return pl.pallas_call(
        level_kernel,
        in_specs=[smem] + [vmem] * 4,
        out_specs=[vmem] * 2,
        out_shape=[shaped(steps, columns, SIDE)] * 2,
        compiler_params=params(),
        cost_estimate=cost(6 * columns * wide * order, 4 * wide * order),
        name="level",
    )(where, upper, lower, *joint)


def fold_kernel(pieces_ref, out_ref):
    count = pieces_ref.shape[0]
    for n in range(count // 2):
        far = count - 1 - n
        out_ref[n, 0:far] = pieces_ref[n, n + 1:count]
        out_ref[n, far] = pieces_ref[n, count]
        for k in range(far + 1, count):
            out_ref[n, k] = pieces_ref[far, k]
        out_ref[n, count] = pieces_ref[far, count]


def fold_of(pieces):
    count = pieces.shape[0]
    return pl.pallas_call(
        fold_kernel,
        in_specs=[vmem],
        out_specs=vmem,
        out_shape=shaped(count // 2, *pieces.shape[1:]),
        compiler_params=params(),
        name="fold",
    )(pieces)


def final_kernel(
    where_ref, own_ref, other_ref, summit_ref, back_ref, reflect_ref, rotated_ref, folded_ref,
    out_ref, solved_ref, coeffs_ref, whole_ref, top_ref, panel_ref, sems, out_sems,
):
    parity = where_ref[0]
    steps = own_ref.shape[0]
    count = 2 * steps
    copies = []
    for p in range(count // 4):
        copy = pltpu.make_async_copy(
            folded_ref.at[:, 2 * p:2 * p + 2], panel_ref.at[p], sems.at[p]
        )
        copy.start()
        copies.append(copy)
    rest = pl.ds(SIDE, rotated_ref.shape[0] - SIDE)
    rest_copy = pltpu.make_async_copy(rotated_ref.at[rest], out_ref.at[rest], out_sems.at[0])
    rest_copy.start()
    for n in range(steps):
        for k, value in enumerate(pick(parity, own_ref[n], other_ref[n])):
            at = pl.ds((2 * n + k) * SIDE, SIDE)
            coeffs_ref[at, :] = value[:SIDE]
            whole_ref[at, :] = value[SIDE:].T
    lowered = thrice(halves(reflect_ref[...]), halves(coeffs_ref[...]))
    lowered = jnp.where(where_ref[2] == 0, back_ref[...], summit_ref[...] - lowered.T)
    top_ref[...] = lowered.T
    top_copy = pltpu.make_async_copy(top_ref, out_ref.at[0:SIDE], out_sems.at[1])
    top_copy.start()

    def block_at(row, column):
        near = min(row, count - 1 - row)
        if row >= count // 2:
            at = column
        else:
            at = count - 1 - row if column == count else column - row - 1
        return panel_ref[near // 2, :, near % 2, at].reshape(SIDE, SIDE)

    zero = jnp.zeros((SIDE, SIDE), jnp.float32)

    def band_of(q, start, stop):
        bands = [
            jnp.concatenate([block_at(k, j) for j in range(start, stop)], axis=1)
            for k in (2 * q, 2 * q + 1)
        ]
        return halves(jnp.concatenate(bands, axis=0))

    last = count // 2 - 1
    solved = [None] * (last + 1)
    ready = whole_ref[pl.ds(2 * last * SIDE, 2 * SIDE), :]
    for q in reversed(range(last + 1)):
        a, b = 2 * q, 2 * q + 1
        if q == last:
            copies[0].wait()
            copies[1].wait()
        inverse = jnp.concatenate(
            [
                jnp.concatenate([block_at(a, count), -block_at(a, b)], axis=1),
                jnp.concatenate([zero, block_at(b, count)], axis=1),
            ],
            axis=0,
        )
        value = ready
        if q < last:
            value = value - thrice(band_of(q, b + 1, b + 3), solved[q + 1])
        value = thrice(halves(inverse), halves(value))
        whole_ref[pl.ds(a * SIDE, 2 * SIDE), :] = value
        solved[q] = halves(value)
        if q > 0:
            ready = whole_ref[pl.ds((a - 2) * SIDE, 2 * SIDE), :]
            if q < last:
                if q - 1 > last // 2:
                    copies[last - q + 1].wait()
                known = [
                    jnp.concatenate([pair[part] for pair in solved[q + 1:]], axis=0)
                    for part in range(2)
                ]
                ready = ready - thrice(band_of(q - 1, b + 1, count), known)
    mine = pl.ds(pl.multiple_of(where_ref[1] * SIDE, SIDE), SIDE)
    solved_ref[...] = whole_ref[mine, :]
    rest_copy.wait()
    top_copy.wait()


def final_of(where, own, other, summit, back, reflect, rotated, folded):
    columns = summit.shape[0]
    order = reflect.shape[1]
    rows, near, long = folded.shape[:3]
    narrow = own.shape[1] - SIDE
    hbm = pl.BlockSpec(memory_space=pltpu.HBM)
    return pl.pallas_call(
        final_kernel,
        in_specs=[smem] + [vmem] * 5 + [hbm] * 2,
        out_specs=[hbm, vmem],
        out_shape=[shaped(*rotated.shape), shaped(SIDE, narrow)],
        scratch_shapes=[
            pltpu.VMEM((order, columns), jnp.float32),
            pltpu.VMEM((order, narrow), jnp.float32),
            pltpu.VMEM((SIDE, columns), jnp.float32),
            pltpu.VMEM((near // 2, rows, 2, long) + folded.shape[3:], jnp.float32),
            pltpu.SemaphoreType.DMA((near // 2,)),
            pltpu.SemaphoreType.DMA((2,)),
        ],
        compiler_params=params(LARGE),
        cost_estimate=cost(8 * columns * order * order, 4 * folded.size),
        name="final",
    )(where, own, other, summit, back, reflect, rotated, folded)


def dot(left, right):
    return jnp.dot(left, right, precision=lax.Precision.HIGHEST, preferred_element_type=jnp.float32)


def moved(value, axis, pairs):
    return lax.ppermute(value, axis, pairs)


def per_device(
    right_side, reflectors, leaf_factor, node_reflect, node_factor, upper_blocks, block_inverse
):
    block = upper_blocks.shape[0]
    columns = right_side.shape[1]
    count = lax.axis_size("leaf")
    rows = lax.axis_size("rows")
    half = count // 2
    row_index = lax.axis_index("rows")
    leaf_index = lax.axis_index("leaf")
    where = jnp.stack([leaf_index % 2, leaf_index, row_index]).astype(jnp.int32)
    swap = [(i, i ^ 1) for i in range(count)]
    same = [list(range(k, count, 2)) for k in range(2)]

    def pair_sum(parts):
        keep, give = parts
        return keep + moved(give, "leaf", swap)

    def scatter_pair(pair):
        got = lax.all_to_all(pair, "leaf", 0, 0, axis_index_groups=same)
        return jnp.sum(got, axis=0)

    def copies(mine):
        return jnp.broadcast_to(mine[None], (half,) + mine.shape)

    def collect(spread):
        own = lax.all_to_all(spread, "leaf", 0, 0, axis_index_groups=same)
        return own, moved(own, "leaf", swap)

    kept = count * 3 // 4 * block
    spare = count * block - kept
    sources = range(count * 3 // 4, count)
    given = moved(node_factor[0, kept:], "leaf", [(k, slot_of(k, count)) for k in sources])
    keep, give = weights_of(where, right_side, reflectors)
    keep, given = lax.optimization_barrier((keep, given))
    factor_whole = lax.all_gather(
        jnp.concatenate(
            [node_factor[0, :kept - spare], node_factor[0, kept - spare:kept] + given], axis=0
        ),
        "leaf",
        axis=0,
    )
    weights_part = scatter_pair(pair_sum((keep, give)))
    spread = coeffs_of(where, *collect(copies(weights_part)), leaf_factor[0])
    rotated, top = lowered_of(where, *collect(spread), reflectors, right_side)

    upper_own, inverse_own = upper_blocks, block_inverse
    inverse_next = moved(inverse_own, "leaf", [(i + 1, i) for i in range(0, count, 2)])
    eighth = block // rows
    upper_slice = lax.dynamic_slice_in_dim(upper_own, row_index * eighth, eighth, 0)
    inverse_slice = lax.dynamic_slice_in_dim(inverse_own, row_index * eighth, eighth, 0)
    upper_slice = upper_slice.reshape(eighth, count, block).transpose(1, 0, 2)
    beside = lax.dynamic_slice_in_dim(
        upper_own, jnp.minimum(leaf_index + 1, count - 1) * block, block, 1
    )
    cross = dot(dot(inverse_slice, beside), inverse_next)
    at_cross = jnp.arange(count)[:, None, None] == leaf_index + 1
    at_cross = jnp.logical_and(at_cross, leaf_index % 2 == 0)
    upper_slice = jnp.where(at_cross, cross[None], upper_slice)
    upper_slice = jnp.concatenate([upper_slice, inverse_slice[None]], axis=0)
    upper_slice, top = lax.optimization_barrier((upper_slice, top))
    pieces = lax.all_gather(upper_slice, "leaf", axis=0)

    joint = joint_of(where, node_reflect[0], factor_whole)

    stride = 1
    upper = top
    lower = moved(top, "rows", [(i, i + 1) for i in range(0, rows, 2)])
    own_coeffs = jnp.zeros_like(top)
    own_top = top
    while stride < rows:
        if stride > 1:
            nodes = list(range(stride, rows, 2 * stride))
            upper = moved(lower, "rows", [(j + stride // 2, j) for j in nodes])
            lower = moved(lower, "rows", [(j - stride // 2, j) for j in nodes])
        share = scatter_pair(pair_sum(level_of(where, upper, lower, joint)))
        if stride == 2:
            share, pieces = lax.optimization_barrier((share, pieces))
            folded = lax.all_gather(fold_of(pieces), "rows", axis=0)
        lower = lower - share
        mine = row_index % (2 * stride) == stride
        own_coeffs = jnp.where(mine, share, own_coeffs)
        own_top = jnp.where(mine, upper, own_top)
        stride *= 2
    root = rows // 2

    back = moved(lower, "rows", [(root, 0)])
    pieces = lower.reshape(rows, columns // rows, block)
    arrived = lax.all_to_all(pieces, "rows", 0, 0)[root]
    own, other = collect(copies(jnp.concatenate([own_coeffs.T, arrived], axis=0)))
    return final_of(where, own, other, own_top, back, node_reflect[0], rotated, folded)


def solution(mesh):
    in_specs = (
        P(("rows", "leaf"), None),
        P(("rows", "leaf"), None),
        P("rows", None, "leaf"),
        P("rows", "leaf", None),
        P("rows", None, "leaf"),
        P("leaf", None),
        P("leaf", None),
    )
    out_specs = (P(("rows", "leaf"), None), P("leaf", "rows"))
    return jax.shard_map(
        per_device, mesh=mesh, in_specs=in_specs, out_specs=out_specs, check_vma=False
    )
```

```python
import functools

import jax
import jax.numpy as jnp
from jax import lax
from jax.experimental import pallas as pl
from jax.experimental.pallas import tpu as pltpu
from jax.sharding import PartitionSpec as P

SIDE = 128
GROUP = 4
SPLIT = (((1,), (0,)), ((), ()))
SMALL = 24 * 1024 * 1024
MEDIUM = 52 * 1024 * 1024
LARGE = 56 * 1024 * 1024


def halves(value):
    high = value.astype(jnp.bfloat16)
    low = (value - high.astype(jnp.float32)).astype(jnp.bfloat16)
    return high, low


def once(left, right):
    return lax.dot_general(left, right, SPLIT, preferred_element_type=jnp.float32)


def thrice(left, right):
    return once(left[0], right[0]) + (once(left[0], right[1]) + once(left[1], right[0]))


def stacked(left, right):
    size = left[0].shape[0]
    both = once(jnp.concatenate(left, axis=0), right[0])
    return both[:size] + (both[size:] + once(left[0], right[1]))


def pick(parity, own, other):
    first = parity == 0
    return jnp.where(first, own, other), jnp.where(first, other, own)


smem = pl.BlockSpec(memory_space=pltpu.SMEM)


vmem = pl.BlockSpec(memory_space=pltpu.VMEM)


def params(limit=SMALL):
    return pltpu.CompilerParams(vmem_limit_bytes=limit)


def cost(flops, size):
    return pl.CostEstimate(flops=flops, bytes_accessed=size, transcendentals=0)


def shaped(*shape, dtype=jnp.float32):
    return jax.ShapeDtypeStruct(shape, dtype)


def weights_kernel(where_ref, side_ref, vectors_ref, keep_ref, give_ref, high_ref, low_ref):
    @pl.when(pl.program_id(0) == 0)
    def _():
        high, low = halves(side_ref[...].T)
        high_ref[...] = high
        low_ref[...] = low

    first = where_ref[0] == 0
    for n in range(keep_ref.shape[0]):
        vectors = vectors_ref[:, 2 * n * SIDE:(2 * n + 2) * SIDE]
        out = stacked((high_ref[...], low_ref[...]), halves(vectors))
        even, odd = out[:, :SIDE], out[:, SIDE:]
        keep_ref[n] = jnp.where(first, even, odd)
        give_ref[n] = jnp.where(first, odd, even)


def weights_of(where, side, vectors):
    tall, order = vectors.shape
    columns = side.shape[1]
    steps = order // (2 * SIDE)
    block = pl.BlockSpec((GROUP, columns, SIDE), lambda n: (n, 0, 0))
    return pl.pallas_call(
        weights_kernel,
        grid=(steps // GROUP,),
        in_specs=[
            smem,
            pl.BlockSpec((tall, columns), lambda n: (0, 0)),
            pl.BlockSpec((tall, 2 * GROUP * SIDE), lambda n: (0, n)),
        ],
        out_specs=[block, block],
        out_shape=[shaped(steps, columns, SIDE)] * 2,
        scratch_shapes=[pltpu.VMEM((columns, tall), jnp.bfloat16)] * 2,
        compiler_params=params(LARGE),
        cost_estimate=cost(6 * tall * columns * order, 4 * vectors.size),
        name="weights",
    )(where, side, vectors)


def coeffs_kernel(where_ref, own_ref, other_ref, factor_ref, out_ref):
    parity = where_ref[0]
    steps = own_ref.shape[0]
    total = jnp.zeros(own_ref.shape[1:], jnp.float32)
    for n in range(steps):
        left = jnp.concatenate(pick(parity, own_ref[n], other_ref[n]), axis=1)
        right = factor_ref[2 * n * SIDE:(2 * n + 2) * SIDE, :]
        total = total + stacked(halves(left), halves(right))
    total = total.T
    for n in range(steps):
        out_ref[n] = total


def coeffs_of(where, own, other, factor):
    return pl.pallas_call(
        coeffs_kernel,
        in_specs=[smem] + [pl.BlockSpec(memory_space=pltpu.VMEM)] * 3,
        out_shape=shaped(own.shape[0], SIDE, own.shape[1]),
        compiler_params=params(),
        cost_estimate=cost(6 * own.shape[1] * factor.size, 4 * factor.size),
        name="coeffs",
    )(where, own, other, factor)


def lowered_kernel(where_ref, own_ref, other_ref, vectors_ref, side_ref, out_ref, top_ref):
    step = pl.program_id(0)

    @pl.when(step == 0)
    def _():
        out_ref[...] = side_ref[...]

    total = out_ref[...]
    for n in range(own_ref.shape[0]):
        right = jnp.concatenate(pick(where_ref[0], own_ref[n], other_ref[n]), axis=0)
        vectors = vectors_ref[:, 2 * n * SIDE:(2 * n + 2) * SIDE]
        total = total - thrice(halves(vectors), halves(right))
    out_ref[...] = total

    @pl.when(step == pl.num_programs(0) - 1)
    def _():
        top_ref[...] = out_ref[:SIDE, :].T


def lowered_of(where, own, other, vectors, side):
    tall, order = vectors.shape
    columns = side.shape[1]
    steps = order // (2 * SIDE)
    block = pl.BlockSpec((GROUP, SIDE, columns), lambda n: (n, 0, 0))
    whole = pl.BlockSpec((tall, columns), lambda n: (0, 0))
    return pl.pallas_call(
        lowered_kernel,
        grid=(steps // GROUP,),
        in_specs=[
            smem, block, block, pl.BlockSpec((tall, 2 * GROUP * SIDE), lambda n: (0, n)), whole,
        ],
        out_specs=[whole, pl.BlockSpec((columns, SIDE), lambda n: (0, 0))],
        out_shape=[shaped(tall, columns), shaped(columns, SIDE)],
        compiler_params=params(LARGE),
        cost_estimate=cost(6 * tall * columns * order, 4 * vectors.size),
        name="lowered",
    )(where, own, other, vectors, side)


def slot_of(k, count):
    return (k + 10) % count if k < count - 2 else k + 2 - count


def joint_kernel(where_ref, reflect_ref, factor_ref, high_ref, low_ref, panel_ref, sems):
    count, kept, _ = factor_ref.shape
    order = reflect_ref.shape[1]
    spare = order - kept
    copies = []
    for k in range(count):
        edge = (k // 2 + 1) * 2 * SIDE
        rows = pl.ds(0, min(edge, kept))
        copies.append(
            [pltpu.make_async_copy(factor_ref.at[k, rows], panel_ref.at[k, rows], sems.at[0, k])]
        )
        if edge > kept:
            copies[k].append(
                pltpu.make_async_copy(
                    factor_ref.at[slot_of(k, count), pl.ds(kept - spare, edge - kept)],
                    panel_ref.at[k, pl.ds(kept, edge - kept)],
                    sems.at[1, k],
                )
            )
        for copy in copies[k]:
            copy.start()
    reflect = halves(reflect_ref[...])
    own = where_ref[1]
    zero = jnp.zeros((SIDE, SIDE), jnp.float32)
    for k in range(0, count, 2):
        for copy in copies[k] + copies[k + 1]:
            copy.wait()
        edge = (k + 2) * SIDE
        panel = jnp.concatenate([panel_ref[k, 0:edge], panel_ref[k + 1, 0:edge]], axis=1)
        top = stacked([r[:, :edge] for r in reflect], halves(panel))
        mine = pl.ds(pl.multiple_of(jnp.minimum(own, k + 1) * SIDE, SIDE), SIDE)
        bottom = [jnp.where(own <= j, panel_ref[j, mine, :], zero) for j in (k, k + 1)]
        bottom = jnp.concatenate(bottom, axis=1)
        at = pl.ds(k * SIDE, 2 * SIDE)
        for ref, first, second in zip((high_ref, low_ref), halves(top), halves(bottom)):
            ref[0:SIDE, at] = first
            ref[SIDE:2 * SIDE, at] = second


def joint_of(where, reflect, factor):
    block, order = reflect.shape
    count = factor.shape[0]
    return pl.pallas_call(
        joint_kernel,
        in_specs=[smem, vmem, pl.BlockSpec(memory_space=pltpu.HBM)],
        out_specs=[vmem] * 2,
        out_shape=[shaped(2 * block, order, dtype=jnp.bfloat16)] * 2,
        scratch_shapes=[
            pltpu.VMEM((count, order, SIDE), jnp.float32),
            pltpu.SemaphoreType.DMA((2, count)),
        ],
        compiler_params=params(MEDIUM),
        cost_estimate=cost(3 * block * order * order, 2 * factor.size),
        name="joint",
    )(where, reflect, factor)


def level_kernel(where_ref, upper_ref, lower_ref, high_ref, low_ref, keep_ref, give_ref):
    first = where_ref[0] == 0
    left = halves(jnp.concatenate([upper_ref[...], lower_ref[...]], axis=1))
    for n in range(keep_ref.shape[0]):
        at = pl.ds(2 * n * SIDE, 2 * SIDE)
        out = stacked(left, (high_ref[:, at], low_ref[:, at]))
        even, odd = out[:, :SIDE], out[:, SIDE:]
        keep_ref[n] = jnp.where(first, even, odd)
        give_ref[n] = jnp.where(first, odd, even)


def level_of(where, upper, lower, joint):
    columns = upper.shape[0]
    wide, order = joint[0].shape
    steps = order // (2 * SIDE)
    return pl.pallas_call(
        level_kernel,
        in_specs=[smem] + [vmem] * 4,
        out_specs=[vmem] * 2,
        out_shape=[shaped(steps, columns, SIDE)] * 2,
        compiler_params=params(),
        cost_estimate=cost(6 * columns * wide * order, 4 * wide * order),
        name="level",
    )(where, upper, lower, *joint)


def fold_kernel(pieces_ref, out_ref):
    count = pieces_ref.shape[0]
    for n in range(count // 2):
        far = count - 1 - n
        out_ref[n, 0:far] = pieces_ref[n, n + 1:count]
        out_ref[n, far] = pieces_ref[n, count]
        for k in range(far + 1, count):
            out_ref[n, k] = pieces_ref[far, k]
        out_ref[n, count] = pieces_ref[far, count]


def fold_of(pieces):
    count = pieces.shape[0]
    return pl.pallas_call(
        fold_kernel,
        in_specs=[vmem],
        out_specs=vmem,
        out_shape=shaped(count // 2, *pieces.shape[1:]),
        compiler_params=params(),
        name="fold",
    )(pieces)


def final_kernel(
    where_ref, own_ref, other_ref, summit_ref, back_ref, reflect_ref, rotated_ref, folded_ref,
    out_ref, solved_ref, coeffs_ref, whole_ref, top_ref, panel_ref, sems, out_sems,
):
    parity = where_ref[0]
    steps = own_ref.shape[0]
    count = 2 * steps
    copies = []
    for p in range(count // 4):
        copy = pltpu.make_async_copy(
            folded_ref.at[:, 2 * p:2 * p + 2], panel_ref.at[p], sems.at[p]
        )
        copy.start()
        copies.append(copy)
    rest = pl.ds(SIDE, rotated_ref.shape[0] - SIDE)
    rest_copy = pltpu.make_async_copy(rotated_ref.at[rest], out_ref.at[rest], out_sems.at[0])
    rest_copy.start()
    for n in range(steps):
        for k, value in enumerate(pick(parity, own_ref[n], other_ref[n])):
            at = pl.ds((2 * n + k) * SIDE, SIDE)
            coeffs_ref[at, :] = value[:SIDE]
            whole_ref[at, :] = value[SIDE:].T
    lowered = thrice(halves(reflect_ref[...]), halves(coeffs_ref[...]))
    lowered = jnp.where(where_ref[2] == 0, back_ref[...], summit_ref[...] - lowered.T)
    top_ref[...] = lowered.T
    top_copy = pltpu.make_async_copy(top_ref, out_ref.at[0:SIDE], out_sems.at[1])
    top_copy.start()

    def block_at(row, column):
        near = min(row, count - 1 - row)
        if row >= count // 2:
            at = column
        else:
            at = count - 1 - row if column == count else column - row - 1
        return panel_ref[near // 2, :, near % 2, at].reshape(SIDE, SIDE)

    zero = jnp.zeros((SIDE, SIDE), jnp.float32)

    def band_of(q, start, stop):
        bands = [
            jnp.concatenate([block_at(k, j) for j in range(start, stop)], axis=1)
            for k in (2 * q, 2 * q + 1)
        ]
        return halves(jnp.concatenate(bands, axis=0))

    last = count // 2 - 1
    solved = [None] * (last + 1)
    ready = whole_ref[pl.ds(2 * last * SIDE, 2 * SIDE), :]
    for q in reversed(range(last + 1)):
        a, b = 2 * q, 2 * q + 1
        if q == last:
            copies[0].wait()
            copies[1].wait()
        inverse = jnp.concatenate(
            [
                jnp.concatenate([block_at(a, count), -block_at(a, b)], axis=1),
                jnp.concatenate([zero, block_at(b, count)], axis=1),
            ],
            axis=0,
        )
        value = ready
        if q < last:
            value = value - thrice(band_of(q, b + 1, b + 3), solved[q + 1])
        value = thrice(halves(inverse), halves(value))
        whole_ref[pl.ds(a * SIDE, 2 * SIDE), :] = value
        solved[q] = halves(value)
        if q > 0:
            ready = whole_ref[pl.ds((a - 2) * SIDE, 2 * SIDE), :]
            if q < last:
                if q - 1 > last // 2:
                    copies[last - q + 1].wait()
                known = [
                    jnp.concatenate([pair[part] for pair in solved[q + 1:]], axis=0)
                    for part in range(2)
                ]
                ready = ready - thrice(band_of(q - 1, b + 1, count), known)
    mine = pl.ds(pl.multiple_of(where_ref[1] * SIDE, SIDE), SIDE)
    solved_ref[...] = whole_ref[mine, :].T
    rest_copy.wait()
    top_copy.wait()


def final_of(where, own, other, summit, back, reflect, rotated, folded):
    columns = summit.shape[0]
    order = reflect.shape[1]
    rows, near, long = folded.shape[:3]
    narrow = own.shape[1] - SIDE
    hbm = pl.BlockSpec(memory_space=pltpu.HBM)
    return pl.pallas_call(
        final_kernel,
        in_specs=[smem] + [vmem] * 5 + [hbm] * 2,
        out_specs=[hbm, vmem],
        out_shape=[shaped(*rotated.shape), shaped(narrow, SIDE)],
        scratch_shapes=[
            pltpu.VMEM((order, columns), jnp.float32),
            pltpu.VMEM((order, narrow), jnp.float32),
            pltpu.VMEM((SIDE, columns), jnp.float32),
            pltpu.VMEM((near // 2, rows, 2, long) + folded.shape[3:], jnp.float32),
            pltpu.SemaphoreType.DMA((near // 2,)),
            pltpu.SemaphoreType.DMA((2,)),
        ],
        compiler_params=params(LARGE),
        cost_estimate=cost(8 * columns * order * order, 4 * folded.size),
        name="final",
    )(where, own, other, summit, back, reflect, rotated, folded)


def dot(left, right):
    return jnp.dot(left, right, precision=lax.Precision.HIGHEST, preferred_element_type=jnp.float32)


def moved(value, axis, pairs):
    return lax.ppermute(value, axis, pairs)


def per_device(
    right_side, reflectors, leaf_factor, node_reflect, node_factor, upper_blocks, block_inverse
):
    block = upper_blocks.shape[0]
    columns = right_side.shape[1]
    count = lax.axis_size("leaf")
    rows = lax.axis_size("rows")
    half = count // 2
    row_index = lax.axis_index("rows")
    leaf_index = lax.axis_index("leaf")
    where = jnp.stack([leaf_index % 2, leaf_index, row_index]).astype(jnp.int32)
    swap = [(i, i ^ 1) for i in range(count)]
    same = [list(range(k, count, 2)) for k in range(2)]

    def pair_sum(parts):
        keep, give = parts
        return keep + moved(give, "leaf", swap)

    def scatter_pair(pair):
        got = lax.all_to_all(pair, "leaf", 0, 0, axis_index_groups=same)
        return jnp.sum(got, axis=0)

    def copies(mine):
        return jnp.broadcast_to(mine[None], (half,) + mine.shape)

    def collect(spread):
        own = lax.all_to_all(spread, "leaf", 0, 0, axis_index_groups=same)
        return own, moved(own, "leaf", swap)

    kept = count * 3 // 4 * block
    spare = count * block - kept
    sources = range(count * 3 // 4, count)
    given = moved(node_factor[0, kept:], "leaf", [(k, slot_of(k, count)) for k in sources])
    keep, give = weights_of(where, right_side, reflectors)
    keep, given = lax.optimization_barrier((keep, given))
    factor_whole = lax.all_gather(
        jnp.concatenate(
            [node_factor[0, :kept - spare], node_factor[0, kept - spare:kept] + given], axis=0
        ),
        "leaf",
        axis=0,
    )
    weights_part = scatter_pair(pair_sum((keep, give)))
    spread = coeffs_of(where, *collect(copies(weights_part)), leaf_factor[0])
    rotated, top = lowered_of(where, *collect(spread), reflectors, right_side)

    upper_own, inverse_own = upper_blocks, block_inverse
    inverse_next = moved(inverse_own, "leaf", [(i + 1, i) for i in range(0, count, 2)])
    eighth = block // rows
    upper_slice = lax.dynamic_slice_in_dim(upper_own, row_index * eighth, eighth, 0)
    inverse_slice = lax.dynamic_slice_in_dim(inverse_own, row_index * eighth, eighth, 0)
    upper_slice = upper_slice.reshape(eighth, count, block).transpose(1, 0, 2)
    beside = lax.dynamic_slice_in_dim(
        upper_own, jnp.minimum(leaf_index + 1, count - 1) * block, block, 1
    )
    cross = dot(dot(inverse_slice, beside), inverse_next)
    at_cross = jnp.arange(count)[:, None, None] == leaf_index + 1
    at_cross = jnp.logical_and(at_cross, leaf_index % 2 == 0)
    upper_slice = jnp.where(at_cross, cross[None], upper_slice)
    upper_slice = jnp.concatenate([upper_slice, inverse_slice[None]], axis=0)
    upper_slice, top = lax.optimization_barrier((upper_slice, top))
    pieces = lax.all_gather(upper_slice, "leaf", axis=0)

    joint = joint_of(where, node_reflect[0], factor_whole)

    stride = 1
    upper = top
    lower = moved(top, "rows", [(i, i + 1) for i in range(0, rows, 2)])
    own_coeffs = jnp.zeros_like(top)
    own_top = top
    while stride < rows:
        if stride > 1:
            nodes = list(range(stride, rows, 2 * stride))
            upper = moved(lower, "rows", [(j + stride // 2, j) for j in nodes])
            lower = moved(lower, "rows", [(j - stride // 2, j) for j in nodes])
        share = scatter_pair(pair_sum(level_of(where, upper, lower, joint)))
        if stride == 2:
            share, pieces = lax.optimization_barrier((share, pieces))
            folded = lax.all_gather(fold_of(pieces), "rows", axis=0)
        lower = lower - share
        mine = row_index % (2 * stride) == stride
        own_coeffs = jnp.where(mine, share, own_coeffs)
        own_top = jnp.where(mine, upper, own_top)
        stride *= 2
    root = rows // 2

    back = moved(lower, "rows", [(root, 0)])
    pieces = lower.reshape(rows, columns // rows, block)
    arrived = lax.all_to_all(pieces, "rows", 0, 0)[root]
    arrived, back = lax.optimization_barrier((arrived, back))
    own, other = collect(copies(jnp.concatenate([own_coeffs.T, arrived], axis=0)))
    rotated, solved = final_of(
        where, own, other, own_top, back, node_reflect[0], rotated, folded
    )
    return (rotated, solved.T)


def solution(mesh):
    in_specs = (
        P(("rows", "leaf"), None),
        P(("rows", "leaf"), None),
        P("rows", None, "leaf"),
        P("rows", "leaf", None),
        P("rows", None, "leaf"),
        P("leaf", None),
        P("leaf", None),
    )
    out_specs = (P(("rows", "leaf"), None), P("leaf", "rows"))
    return jax.shard_map(
        per_device, mesh=mesh, in_specs=in_specs, out_specs=out_specs, check_vma=False
    )
```

```python
import functools

import jax
import jax.numpy as jnp
from jax import lax
from jax.experimental import pallas as pl
from jax.experimental.pallas import tpu as pltpu
from jax.sharding import PartitionSpec as P

SIDE = 128
GROUP = 4
SPLIT = (((1,), (0,)), ((), ()))
SMALL = 24 * 1024 * 1024
MEDIUM = 51 * 1024 * 1024
LARGE = 56 * 1024 * 1024


def halves(value):
    high = value.astype(jnp.bfloat16)
    low = (value - high.astype(jnp.float32)).astype(jnp.bfloat16)
    return high, low


def once(left, right):
    return lax.dot_general(left, right, SPLIT, preferred_element_type=jnp.float32)


def crossed(left, right):
    return lax.dot_general(
        left, right, (((1,), (1,)), ((), ())), preferred_element_type=jnp.float32
    )


def thrice(left, right):
    return once(left[0], right[0]) + (once(left[0], right[1]) + once(left[1], right[0]))


def stacked(left, right):
    size = left[0].shape[0]
    both = once(jnp.concatenate(left, axis=0), right[0])
    return both[:size] + (both[size:] + once(left[0], right[1]))


def pick(parity, own, other):
    first = parity == 0
    return jnp.where(first, own, other), jnp.where(first, other, own)


smem = pl.BlockSpec(memory_space=pltpu.SMEM)


vmem = pl.BlockSpec(memory_space=pltpu.VMEM)


def params(limit=SMALL):
    return pltpu.CompilerParams(vmem_limit_bytes=limit)


def cost(flops, size):
    return pl.CostEstimate(flops=flops, bytes_accessed=size, transcendentals=0)


def shaped(*shape, dtype=jnp.float32):
    return jax.ShapeDtypeStruct(shape, dtype)


def weights_kernel(where_ref, side_ref, vectors_ref, keep_ref, give_ref, high_ref, low_ref):
    @pl.when(pl.program_id(0) == 0)
    def _():
        high, low = halves(side_ref[...].T)
        high_ref[...] = high
        low_ref[...] = low

    first = where_ref[0] == 0
    for n in range(keep_ref.shape[0]):
        vectors = vectors_ref[:, 2 * n * SIDE:(2 * n + 2) * SIDE]
        out = stacked((high_ref[...], low_ref[...]), halves(vectors))
        even, odd = out[:, :SIDE], out[:, SIDE:]
        keep_ref[n] = jnp.where(first, even, odd)
        give_ref[n] = jnp.where(first, odd, even)


def weights_of(where, side, vectors):
    tall, order = vectors.shape
    columns = side.shape[1]
    steps = order // (2 * SIDE)
    block = pl.BlockSpec((GROUP, columns, SIDE), lambda n: (n, 0, 0))
    return pl.pallas_call(
        weights_kernel,
        grid=(steps // GROUP,),
        in_specs=[
            smem,
            pl.BlockSpec((tall, columns), lambda n: (0, 0)),
            pl.BlockSpec((tall, 2 * GROUP * SIDE), lambda n: (0, n)),
        ],
        out_specs=[block, block],
        out_shape=[shaped(steps, columns, SIDE)] * 2,
        scratch_shapes=[pltpu.VMEM((columns, tall), jnp.bfloat16)] * 2,
        compiler_params=params(LARGE),
        cost_estimate=cost(6 * tall * columns * order, 4 * vectors.size),
        name="weights",
    )(where, side, vectors)


def coeffs_kernel(where_ref, own_ref, other_ref, factor_ref, out_ref):
    parity = where_ref[0]
    steps = own_ref.shape[0]
    total = jnp.zeros(own_ref.shape[1:], jnp.float32)
    for n in range(steps):
        left = jnp.concatenate(pick(parity, own_ref[n], other_ref[n]), axis=1)
        right = factor_ref[2 * n * SIDE:(2 * n + 2) * SIDE, :]
        total = total + stacked(halves(left), halves(right))
    total = total.T
    for n in range(steps):
        out_ref[n] = total


def coeffs_of(where, own, other, factor):
    return pl.pallas_call(
        coeffs_kernel,
        in_specs=[smem] + [pl.BlockSpec(memory_space=pltpu.VMEM)] * 3,
        out_shape=shaped(own.shape[0], SIDE, own.shape[1]),
        compiler_params=params(),
        cost_estimate=cost(6 * own.shape[1] * factor.size, 4 * factor.size),
        name="coeffs",
    )(where, own, other, factor)


def lowered_kernel(where_ref, own_ref, other_ref, vectors_ref, side_ref, out_ref, top_ref):
    step = pl.program_id(0)

    @pl.when(step == 0)
    def _():
        out_ref[...] = side_ref[...]

    total = out_ref[...]
    for n in range(own_ref.shape[0]):
        right = jnp.concatenate(pick(where_ref[0], own_ref[n], other_ref[n]), axis=0)
        vectors = vectors_ref[:, 2 * n * SIDE:(2 * n + 2) * SIDE]
        total = total - thrice(halves(vectors), halves(right))
    out_ref[...] = total

    @pl.when(step == pl.num_programs(0) - 1)
    def _():
        top_ref[...] = out_ref[:SIDE, :].T


def lowered_of(where, own, other, vectors, side):
    tall, order = vectors.shape
    columns = side.shape[1]
    steps = order // (2 * SIDE)
    block = pl.BlockSpec((GROUP, SIDE, columns), lambda n: (n, 0, 0))
    whole = pl.BlockSpec((tall, columns), lambda n: (0, 0))
    return pl.pallas_call(
        lowered_kernel,
        grid=(steps // GROUP,),
        in_specs=[
            smem, block, block, pl.BlockSpec((tall, 2 * GROUP * SIDE), lambda n: (0, n)), whole,
        ],
        out_specs=[whole, pl.BlockSpec((columns, SIDE), lambda n: (0, 0))],
        out_shape=[shaped(tall, columns), shaped(columns, SIDE)],
        compiler_params=params(LARGE),
        cost_estimate=cost(6 * tall * columns * order, 4 * vectors.size),
        name="lowered",
    )(where, own, other, vectors, side)


KEPT = 10
ENDS = {10: (6, 8), 11: (7, 8), 12: (4, 6), 13: (5, 6), 14: (0, 4), 15: (1, 4)}


def joint_kernel(where_ref, reflect_ref, factor_ref, high_ref, low_ref, panel_ref, sems):
    count, kept, _ = factor_ref.shape
    copies = [None] * count
    for k in reversed(range(count)):
        edge = (k // 2 + 1) * 2 * SIDE
        rows = pl.ds(0, min(edge, kept))
        copies[k] = [
            pltpu.make_async_copy(factor_ref.at[k, rows], panel_ref.at[k, rows], sems.at[0, k])
        ]
        if edge > kept:
            slot, first = ENDS[k]
            copies[k].append(
                pltpu.make_async_copy(
                    factor_ref.at[slot, pl.ds(first * SIDE, edge - kept)],
                    panel_ref.at[k, pl.ds(kept, edge - kept)],
                    sems.at[1, k],
                )
            )
        for copy in copies[k]:
            copy.start()
    reflect = halves(reflect_ref[...])
    own = where_ref[1]
    zero = jnp.zeros((SIDE, SIDE), jnp.float32)
    for k in reversed(range(0, count, 2)):
        for copy in copies[k] + copies[k + 1]:
            copy.wait()
        edge = (k + 2) * SIDE
        panel = jnp.concatenate([panel_ref[k, 0:edge], panel_ref[k + 1, 0:edge]], axis=1)
        top = stacked([r[:, :edge] for r in reflect], halves(panel))
        mine = pl.ds(pl.multiple_of(jnp.minimum(own, k + 1) * SIDE, SIDE), SIDE)
        bottom = [jnp.where(own <= j, panel_ref[j, mine, :], zero) for j in (k, k + 1)]
        bottom = jnp.concatenate(bottom, axis=1)
        at = pl.ds(k * SIDE, 2 * SIDE)
        for ref, first, second in zip((high_ref, low_ref), halves(top), halves(bottom)):
            ref[0:SIDE, at] = first
            ref[SIDE:2 * SIDE, at] = second


def joint_of(where, reflect, factor):
    block, order = reflect.shape
    count = factor.shape[0]
    return pl.pallas_call(
        joint_kernel,
        in_specs=[smem, vmem, pl.BlockSpec(memory_space=pltpu.HBM)],
        out_specs=[vmem] * 2,
        out_shape=[shaped(2 * block, order, dtype=jnp.bfloat16)] * 2,
        scratch_shapes=[
            pltpu.VMEM((count, order, SIDE), jnp.float32),
            pltpu.SemaphoreType.DMA((2, count)),
        ],
        compiler_params=params(MEDIUM),
        cost_estimate=cost(3 * block * order * order, 2 * factor.size),
        name="joint",
    )(where, reflect, factor)


def level_kernel(where_ref, upper_ref, lower_ref, high_ref, low_ref, keep_ref, give_ref):
    first = where_ref[0] == 0
    left = halves(jnp.concatenate([upper_ref[...], lower_ref[...]], axis=1))
    for n in range(keep_ref.shape[0]):
        at = pl.ds(2 * n * SIDE, 2 * SIDE)
        out = stacked(left, (high_ref[:, at], low_ref[:, at]))
        even, odd = out[:, :SIDE], out[:, SIDE:]
        keep_ref[n] = jnp.where(first, even, odd)
        give_ref[n] = jnp.where(first, odd, even)


def level_of(where, upper, lower, joint):
    columns = upper.shape[0]
    wide, order = joint[0].shape
    steps = order // (2 * SIDE)
    return pl.pallas_call(
        level_kernel,
        in_specs=[smem] + [vmem] * 4,
        out_specs=[vmem] * 2,
        out_shape=[shaped(steps, columns, SIDE)] * 2,
        compiler_params=params(),
        cost_estimate=cost(6 * columns * wide * order, 4 * wide * order),
        name="level",
    )(where, upper, lower, *joint)


def fold_kernel(pieces_ref, out_ref):
    count = pieces_ref.shape[0]
    for n in range(count // 2):
        far = count - 1 - n
        out_ref[n, 0:far] = pieces_ref[n, n + 1:count]
        out_ref[n, far] = pieces_ref[n, count]
        for k in range(far + 1, count):
            out_ref[n, k] = pieces_ref[far, k]
        out_ref[n, count] = pieces_ref[far, count]


def fold_of(pieces):
    count = pieces.shape[0]
    return pl.pallas_call(
        fold_kernel,
        in_specs=[vmem],
        out_specs=vmem,
        out_shape=shaped(count // 2, *pieces.shape[1:]),
        compiler_params=params(),
        name="fold",
    )(pieces)


def final_kernel(
    where_ref, own_ref, other_ref, summit_ref, back_ref, reflect_ref, rotated_ref, folded_ref,
    out_ref, solved_ref, coeffs_ref, whole_ref, top_ref, panel_ref, sems, out_sems,
):
    parity = where_ref[0]
    steps = own_ref.shape[0]
    count = 2 * steps
    copies = []
    for p in range(count // 4):
        copy = pltpu.make_async_copy(
            folded_ref.at[:, 2 * p:2 * p + 2], panel_ref.at[p], sems.at[p]
        )
        copy.start()
        copies.append(copy)
    rest = pl.ds(SIDE, rotated_ref.shape[0] - SIDE)
    rest_copy = pltpu.make_async_copy(rotated_ref.at[rest], out_ref.at[rest], out_sems.at[0])
    rest_copy.start()
    for n in range(steps):
        for k, value in enumerate(pick(parity, own_ref[n], other_ref[n])):
            at = pl.ds((2 * n + k) * SIDE, SIDE)
            coeffs_ref[at, :] = value[:SIDE]
            whole_ref[:, at] = value[SIDE:]
    lowered = thrice(halves(reflect_ref[...]), halves(coeffs_ref[...]))
    lowered = jnp.where(where_ref[2] == 0, back_ref[...], summit_ref[...] - lowered.T)
    top_ref[...] = lowered.T
    top_copy = pltpu.make_async_copy(top_ref, out_ref.at[0:SIDE], out_sems.at[1])
    top_copy.start()

    def block_at(row, column):
        near = min(row, count - 1 - row)
        if row >= count // 2:
            at = column
        else:
            at = count - 1 - row if column == count else column - row - 1
        return panel_ref[near // 2, :, near % 2, at].reshape(SIDE, SIDE)

    zero = jnp.zeros((SIDE, SIDE), jnp.float32)

    def band_of(q, start, stop):
        bands = [
            jnp.concatenate([block_at(k, j) for j in range(start, stop)], axis=1)
            for k in (2 * q, 2 * q + 1)
        ]
        return halves(jnp.concatenate(bands, axis=0))

    def parts_of(value):
        high = value.astype(jnp.bfloat16).astype(jnp.float32)
        return jnp.concatenate([high, value - high], axis=0).astype(jnp.bfloat16)

    def across(parts, right):
        both = crossed(parts, right[0]) + crossed(parts, right[1])
        size = both.shape[0] // 2
        return both[:size] + both[size:]

    last = count // 2 - 1
    known = None
    ready = whole_ref[:, pl.ds(2 * last * SIDE, 2 * SIDE)]
    for q in reversed(range(last + 1)):
        a, b = 2 * q, 2 * q + 1
        if q == last:
            copies[0].wait()
            copies[1].wait()
        inverse = jnp.concatenate(
            [
                jnp.concatenate([block_at(a, count), -block_at(a, b)], axis=1),
                jnp.concatenate([zero, block_at(b, count)], axis=1),
            ],
            axis=0,
        )
        value = ready
        if q < last:
            value = value - across(newest, band_of(q, b + 1, b + 3))
        value = across(parts_of(value), halves(inverse))
        whole_ref[:, pl.ds(a * SIDE, 2 * SIDE)] = value
        newest = parts_of(value)
        known = newest if known is None else jnp.concatenate([newest, known], axis=1)
        if q > 0:
            ready = whole_ref[:, pl.ds((a - 2) * SIDE, 2 * SIDE)]
            if q < last:
                if q - 1 > last // 2:
                    copies[last - q + 1].wait()
                ready = ready - across(known[:, 2 * SIDE:], band_of(q - 1, b + 1, count))
    mine = pl.ds(pl.multiple_of(where_ref[1] * SIDE, SIDE), SIDE)
    solved_ref[...] = whole_ref[:, mine]
    rest_copy.wait()
    top_copy.wait()


def final_of(where, own, other, summit, back, reflect, rotated, folded):
    columns = summit.shape[0]
    order = reflect.shape[1]
    rows, near, long = folded.shape[:3]
    narrow = own.shape[1] - SIDE
    hbm = pl.BlockSpec(memory_space=pltpu.HBM)
    return pl.pallas_call(
        final_kernel,
        in_specs=[smem] + [vmem] * 5 + [hbm] * 2,
        out_specs=[hbm, vmem],
        out_shape=[shaped(*rotated.shape), shaped(narrow, SIDE)],
        scratch_shapes=[
            pltpu.VMEM((order, columns), jnp.float32),
            pltpu.VMEM((narrow, order), jnp.float32),
            pltpu.VMEM((SIDE, columns), jnp.float32),
            pltpu.VMEM((near // 2, rows, 2, long) + folded.shape[3:], jnp.float32),
            pltpu.SemaphoreType.DMA((near // 2,)),
            pltpu.SemaphoreType.DMA((2,)),
        ],
        compiler_params=params(LARGE),
        cost_estimate=cost(8 * columns * order * order, 4 * folded.size),
        name="final",
    )(where, own, other, summit, back, reflect, rotated, folded)


def dot(left, right):
    return jnp.dot(left, right, precision=lax.Precision.HIGHEST, preferred_element_type=jnp.float32)


def moved(value, axis, pairs):
    return lax.ppermute(value, axis, pairs)


def per_device(
    right_side, reflectors, leaf_factor, node_reflect, node_factor, upper_blocks, block_inverse
):
    block = upper_blocks.shape[0]
    columns = right_side.shape[1]
    count = lax.axis_size("leaf")
    rows = lax.axis_size("rows")
    half = count // 2
    row_index = lax.axis_index("rows")
    leaf_index = lax.axis_index("leaf")
    where = jnp.stack([leaf_index % 2, leaf_index, row_index]).astype(jnp.int32)
    swap = [(i, i ^ 1) for i in range(count)]
    same = [list(range(k, count, 2)) for k in range(2)]

    def pair_sum(parts):
        keep, give = parts
        return keep + moved(give, "leaf", swap)

    def scatter_pair(pair):
        got = lax.all_to_all(pair, "leaf", 0, 0, axis_index_groups=same)
        return jnp.sum(got, axis=0)

    def copies(mine):
        return jnp.broadcast_to(mine[None], (half,) + mine.shape)

    def collect(spread):
        own = lax.all_to_all(spread, "leaf", 0, 0, axis_index_groups=same)
        return own, moved(own, "leaf", swap)

    start = KEPT * block
    longest = moved(
        node_factor[0, start:], "leaf", [(k, ENDS[k][0]) for k in (14, 15)]
    )
    longer = moved(
        node_factor[0, start:start + 4 * block], "leaf", [(k, ENDS[k][0]) for k in (10, 11, 12, 13)]
    )
    keep, give = weights_of(where, right_side, reflectors)
    keep, longest, longer = lax.optimization_barrier((keep, longest, longer))

    def lowered_by(value, first):
        return jnp.pad(value, ((first * block, start - first * block - value.shape[0]), (0, 0)))

    longer = jnp.where(
        leaf_index < ENDS[10][0],
        lowered_by(longer, ENDS[12][1]),
        lowered_by(longer[:2 * block], ENDS[10][1]),
    )
    factor_whole = lax.all_gather(
        node_factor[0, :start] + (lowered_by(longest, ENDS[14][1]) + longer), "leaf", axis=0
    )
    weights_part = scatter_pair(pair_sum((keep, give)))
    spread = coeffs_of(where, *collect(copies(weights_part)), leaf_factor[0])
    rotated, top = lowered_of(where, *collect(spread), reflectors, right_side)

    upper_own, inverse_own = upper_blocks, block_inverse
    inverse_next = moved(inverse_own, "leaf", [(i + 1, i) for i in range(0, count, 2)])
    eighth = block // rows
    upper_slice = lax.dynamic_slice_in_dim(upper_own, row_index * eighth, eighth, 0)
    inverse_slice = lax.dynamic_slice_in_dim(inverse_own, row_index * eighth, eighth, 0)
    upper_slice = upper_slice.reshape(eighth, count, block).transpose(1, 0, 2)
    beside = lax.dynamic_slice_in_dim(
        upper_own, jnp.minimum(leaf_index + 1, count - 1) * block, block, 1
    )
    cross = dot(dot(inverse_slice, beside), inverse_next)
    at_cross = jnp.arange(count)[:, None, None] == leaf_index + 1
    at_cross = jnp.logical_and(at_cross, leaf_index % 2 == 0)
    upper_slice = jnp.where(at_cross, cross[None], upper_slice)
    upper_slice = jnp.concatenate([upper_slice, inverse_slice[None]], axis=0)
    upper_slice, top = lax.optimization_barrier((upper_slice, top))
    pieces = lax.all_gather(upper_slice, "leaf", axis=0)

    joint = joint_of(where, node_reflect[0], factor_whole)

    stride = 1
    upper = top
    lower = moved(top, "rows", [(i, i + 1) for i in range(0, rows, 2)])
    own_coeffs = jnp.zeros_like(top)
    own_top = top
    while stride < rows:
        if stride > 1:
            nodes = list(range(stride, rows, 2 * stride))
            upper = moved(lower, "rows", [(j + stride // 2, j) for j in nodes])
            lower = moved(lower, "rows", [(j - stride // 2, j) for j in nodes])
        share = scatter_pair(pair_sum(level_of(where, upper, lower, joint)))
        if stride == 2:
            share, pieces = lax.optimization_barrier((share, pieces))
            folded = lax.all_gather(fold_of(pieces), "rows", axis=0)
        lower = lower - share
        mine = row_index % (2 * stride) == stride
        own_coeffs = jnp.where(mine, share, own_coeffs)
        own_top = jnp.where(mine, upper, own_top)
        stride *= 2
    root = rows // 2

    back = moved(lower, "rows", [(root, 0)])
    pieces = lower.reshape(rows, columns // rows, block)
    arrived = lax.all_to_all(pieces, "rows", 0, 0)[root]
    arrived, back = lax.optimization_barrier((arrived, back))
    own, other = collect(copies(jnp.concatenate([own_coeffs.T, arrived], axis=0)))
    rotated, solved = final_of(
        where, own, other, own_top, back, node_reflect[0], rotated, folded
    )
    return (rotated, solved.T)


def solution(mesh):
    in_specs = (
        P(("rows", "leaf"), None),
        P(("rows", "leaf"), None),
        P("rows", None, "leaf"),
        P("rows", "leaf", None),
        P("rows", None, "leaf"),
        P("leaf", None),
        P("leaf", None),
    )
    out_specs = (P(("rows", "leaf"), None), P("leaf", "rows"))
    return jax.shard_map(
        per_device, mesh=mesh, in_specs=in_specs, out_specs=out_specs, check_vma=False
    )
```

```python
import functools

import jax
import jax.numpy as jnp
from jax import lax
from jax.experimental import pallas as pl
from jax.experimental.pallas import tpu as pltpu
from jax.sharding import PartitionSpec as P

SIDE = 128
GROUP = 4
SPLIT = (((1,), (0,)), ((), ()))
SMALL = 24 * 1024 * 1024
MEDIUM = 51 * 1024 * 1024
LARGE = 56 * 1024 * 1024


def halves(value):
    high = value.astype(jnp.bfloat16)
    low = (value - high.astype(jnp.float32)).astype(jnp.bfloat16)
    return high, low


def once(left, right):
    return lax.dot_general(left, right, SPLIT, preferred_element_type=jnp.float32)


def crossed(left, right):
    return lax.dot_general(
        left, right, (((1,), (1,)), ((), ())), preferred_element_type=jnp.float32
    )


def thrice(left, right):
    return once(left[0], right[0]) + (once(left[0], right[1]) + once(left[1], right[0]))


def stacked(left, right):
    size = left[0].shape[0]
    both = once(jnp.concatenate(left, axis=0), right[0])
    return both[:size] + (both[size:] + once(left[0], right[1]))


def pick(parity, own, other):
    first = parity == 0
    return jnp.where(first, own, other), jnp.where(first, other, own)


smem = pl.BlockSpec(memory_space=pltpu.SMEM)


vmem = pl.BlockSpec(memory_space=pltpu.VMEM)


def params(limit=SMALL):
    return pltpu.CompilerParams(vmem_limit_bytes=limit)


def cost(flops, size):
    return pl.CostEstimate(flops=flops, bytes_accessed=size, transcendentals=0)


def shaped(*shape, dtype=jnp.float32):
    return jax.ShapeDtypeStruct(shape, dtype)


def weights_kernel(where_ref, side_ref, vectors_ref, keep_ref, give_ref, high_ref, low_ref):
    @pl.when(pl.program_id(0) == 0)
    def _():
        high, low = halves(side_ref[...].T)
        high_ref[...] = high
        low_ref[...] = low

    first = where_ref[0] == 0
    for n in range(keep_ref.shape[0]):
        vectors = vectors_ref[:, 2 * n * SIDE:(2 * n + 2) * SIDE]
        out = stacked((high_ref[...], low_ref[...]), halves(vectors))
        even, odd = out[:, :SIDE], out[:, SIDE:]
        keep_ref[n] = jnp.where(first, even, odd)
        give_ref[n] = jnp.where(first, odd, even)


def weights_of(where, side, vectors):
    tall, order = vectors.shape
    columns = side.shape[1]
    steps = order // (2 * SIDE)
    block = pl.BlockSpec((GROUP, columns, SIDE), lambda n: (n, 0, 0))
    return pl.pallas_call(
        weights_kernel,
        grid=(steps // GROUP,),
        in_specs=[
            smem,
            pl.BlockSpec((tall, columns), lambda n: (0, 0)),
            pl.BlockSpec((tall, 2 * GROUP * SIDE), lambda n: (0, n)),
        ],
        out_specs=[block, block],
        out_shape=[shaped(steps, columns, SIDE)] * 2,
        scratch_shapes=[pltpu.VMEM((columns, tall), jnp.bfloat16)] * 2,
        compiler_params=params(LARGE),
        cost_estimate=cost(6 * tall * columns * order, 4 * vectors.size),
        name="weights",
    )(where, side, vectors)


def coeffs_kernel(where_ref, own_ref, other_ref, factor_ref, out_ref):
    parity = where_ref[0]
    steps = own_ref.shape[0]
    total = jnp.zeros(own_ref.shape[1:], jnp.float32)
    for n in range(steps):
        left = jnp.concatenate(pick(parity, own_ref[n], other_ref[n]), axis=1)
        right = factor_ref[2 * n * SIDE:(2 * n + 2) * SIDE, :]
        total = total + stacked(halves(left), halves(right))
    total = total.T
    for n in range(steps):
        out_ref[n] = total


def coeffs_of(where, own, other, factor):
    return pl.pallas_call(
        coeffs_kernel,
        in_specs=[smem] + [pl.BlockSpec(memory_space=pltpu.VMEM)] * 3,
        out_shape=shaped(own.shape[0], SIDE, own.shape[1]),
        compiler_params=params(),
        cost_estimate=cost(6 * own.shape[1] * factor.size, 4 * factor.size),
        name="coeffs",
    )(where, own, other, factor)


def lowered_kernel(where_ref, own_ref, other_ref, vectors_ref, side_ref, out_ref, top_ref):
    step = pl.program_id(0)

    @pl.when(step == 0)
    def _():
        out_ref[...] = side_ref[...]

    total = out_ref[...]
    for n in range(own_ref.shape[0]):
        right = jnp.concatenate(pick(where_ref[0], own_ref[n], other_ref[n]), axis=0)
        vectors = vectors_ref[:, 2 * n * SIDE:(2 * n + 2) * SIDE]
        total = total - thrice(halves(vectors), halves(right))
    out_ref[...] = total

    @pl.when(step == pl.num_programs(0) - 1)
    def _():
        top_ref[...] = out_ref[:SIDE, :].T


def lowered_of(where, own, other, vectors, side):
    tall, order = vectors.shape
    columns = side.shape[1]
    steps = order // (2 * SIDE)
    block = pl.BlockSpec((GROUP, SIDE, columns), lambda n: (n, 0, 0))
    whole = pl.BlockSpec((tall, columns), lambda n: (0, 0))
    return pl.pallas_call(
        lowered_kernel,
        grid=(steps // GROUP,),
        in_specs=[
            smem, block, block, pl.BlockSpec((tall, 2 * GROUP * SIDE), lambda n: (0, n)), whole,
        ],
        out_specs=[whole, pl.BlockSpec((columns, SIDE), lambda n: (0, 0))],
        out_shape=[shaped(tall, columns), shaped(columns, SIDE)],
        compiler_params=params(LARGE),
        cost_estimate=cost(6 * tall * columns * order, 4 * vectors.size),
        name="lowered",
    )(where, own, other, vectors, side)


KEPT = 10
ENDS = {10: (6, 8), 11: (7, 8), 12: (4, 6), 13: (5, 6), 14: (0, 4), 15: (1, 4)}


def joint_kernel(where_ref, reflect_ref, factor_ref, high_ref, low_ref, panel_ref, sems):
    count, kept, _ = factor_ref.shape
    copies = [None] * count
    for k in reversed(range(count)):
        edge = (k // 2 + 1) * 2 * SIDE
        rows = pl.ds(0, min(edge, kept))
        copies[k] = [
            pltpu.make_async_copy(factor_ref.at[k, rows], panel_ref.at[k, rows], sems.at[0, k])
        ]
        if edge > kept:
            slot, first = ENDS[k]
            copies[k].append(
                pltpu.make_async_copy(
                    factor_ref.at[slot, pl.ds(first * SIDE, edge - kept)],
                    panel_ref.at[k, pl.ds(kept, edge - kept)],
                    sems.at[1, k],
                )
            )
        for copy in copies[k]:
            copy.start()
    reflect = halves(reflect_ref[...])
    own = where_ref[1]
    zero = jnp.zeros((SIDE, SIDE), jnp.float32)
    for k in reversed(range(0, count, 2)):
        for copy in copies[k] + copies[k + 1]:
            copy.wait()
        edge = (k + 2) * SIDE
        panel = jnp.concatenate([panel_ref[k, 0:edge], panel_ref[k + 1, 0:edge]], axis=1)
        top = stacked([r[:, :edge] for r in reflect], halves(panel))
        mine = pl.ds(pl.multiple_of(jnp.minimum(own, k + 1) * SIDE, SIDE), SIDE)
        bottom = [jnp.where(own <= j, panel_ref[j, mine, :], zero) for j in (k, k + 1)]
        bottom = jnp.concatenate(bottom, axis=1)
        at = pl.ds(k * SIDE, 2 * SIDE)
        for ref, first, second in zip((high_ref, low_ref), halves(top), halves(bottom)):
            ref[0:SIDE, at] = first
            ref[SIDE:2 * SIDE, at] = second


def joint_of(where, reflect, factor):
    block, order = reflect.shape
    count = factor.shape[0]
    return pl.pallas_call(
        joint_kernel,
        in_specs=[smem, vmem, pl.BlockSpec(memory_space=pltpu.HBM)],
        out_specs=[vmem] * 2,
        out_shape=[shaped(2 * block, order, dtype=jnp.bfloat16)] * 2,
        scratch_shapes=[
            pltpu.VMEM((count, order, SIDE), jnp.float32),
            pltpu.SemaphoreType.DMA((2, count)),
        ],
        compiler_params=params(MEDIUM),
        cost_estimate=cost(3 * block * order * order, 2 * factor.size),
        name="joint",
    )(where, reflect, factor)


def level_kernel(where_ref, upper_ref, lower_ref, high_ref, low_ref, keep_ref, give_ref):
    first = where_ref[0] == 0
    left = halves(jnp.concatenate([upper_ref[...], lower_ref[...]], axis=1))
    for n in range(keep_ref.shape[0]):
        at = pl.ds(2 * n * SIDE, 2 * SIDE)
        out = stacked(left, (high_ref[:, at], low_ref[:, at]))
        even, odd = out[:, :SIDE], out[:, SIDE:]
        keep_ref[n] = jnp.where(first, even, odd)
        give_ref[n] = jnp.where(first, odd, even)


def level_of(where, upper, lower, joint):
    columns = upper.shape[0]
    wide, order = joint[0].shape
    steps = order // (2 * SIDE)
    return pl.pallas_call(
        level_kernel,
        in_specs=[smem] + [vmem] * 4,
        out_specs=[vmem] * 2,
        out_shape=[shaped(steps, columns, SIDE)] * 2,
        compiler_params=params(),
        cost_estimate=cost(6 * columns * wide * order, 4 * wide * order),
        name="level",
    )(where, upper, lower, *joint)


def fold_kernel(pieces_ref, after_ref, out_ref):
    count = pieces_ref.shape[0]
    for n in range(count // 2):
        far = count - 1 - n
        out_ref[n, 0:far] = pieces_ref[n, n + 1:count]
        out_ref[n, far] = pieces_ref[n, count]
        for k in range(far + 1, count):
            out_ref[n, k] = pieces_ref[far, k]
        out_ref[n, count] = pieces_ref[far, count]


def fold_of(pieces, after):
    count = pieces.shape[0]
    return pl.pallas_call(
        fold_kernel,
        in_specs=[vmem, vmem],
        out_specs=vmem,
        out_shape=shaped(count // 2, *pieces.shape[1:]),
        compiler_params=params(),
        name="fold",
    )(pieces, after)


def final_kernel(
    where_ref, own_ref, other_ref, summit_ref, back_ref, reflect_ref, rotated_ref, folded_ref,
    out_ref, solved_ref, coeffs_ref, whole_ref, top_ref, panel_ref, sems, out_sems,
):
    parity = where_ref[0]
    steps = own_ref.shape[0]
    count = 2 * steps
    copies = []
    for p in range(count // 4):
        copy = pltpu.make_async_copy(
            folded_ref.at[:, 2 * p:2 * p + 2], panel_ref.at[p], sems.at[p]
        )
        copy.start()
        copies.append(copy)
    rest = pl.ds(SIDE, rotated_ref.shape[0] - SIDE)
    rest_copy = pltpu.make_async_copy(rotated_ref.at[rest], out_ref.at[rest], out_sems.at[0])
    rest_copy.start()
    for n in range(steps):
        for k, value in enumerate(pick(parity, own_ref[n], other_ref[n])):
            at = pl.ds((2 * n + k) * SIDE, SIDE)
            coeffs_ref[at, :] = value[:SIDE]
            whole_ref[:, at] = value[SIDE:]
    lowered = thrice(halves(reflect_ref[...]), halves(coeffs_ref[...]))
    lowered = jnp.where(where_ref[2] == 0, back_ref[...], summit_ref[...] - lowered.T)
    top_ref[...] = lowered.T
    top_copy = pltpu.make_async_copy(top_ref, out_ref.at[0:SIDE], out_sems.at[1])
    top_copy.start()

    def block_at(row, column):
        near = min(row, count - 1 - row)
        if row >= count // 2:
            at = column
        else:
            at = count - 1 - row if column == count else column - row - 1
        return panel_ref[near // 2, :, near % 2, at].reshape(SIDE, SIDE)

    zero = jnp.zeros((SIDE, SIDE), jnp.float32)

    def band_of(q, start, stop):
        bands = [
            jnp.concatenate([block_at(k, j) for j in range(start, stop)], axis=1)
            for k in (2 * q, 2 * q + 1)
        ]
        return halves(jnp.concatenate(bands, axis=0))

    def parts_of(value):
        high = value.astype(jnp.bfloat16).astype(jnp.float32)
        return jnp.concatenate([high, value - high], axis=0).astype(jnp.bfloat16)

    def across(parts, right):
        both = crossed(parts, right[0]) + crossed(parts, right[1])
        size = both.shape[0] // 2
        return both[:size] + both[size:]

    last = count // 2 - 1
    known = None
    ready = whole_ref[:, pl.ds(2 * last * SIDE, 2 * SIDE)]
    for q in reversed(range(last + 1)):
        a, b = 2 * q, 2 * q + 1
        if q == last:
            copies[0].wait()
            copies[1].wait()
        inverse = jnp.concatenate(
            [
                jnp.concatenate([block_at(a, count), -block_at(a, b)], axis=1),
                jnp.concatenate([zero, block_at(b, count)], axis=1),
            ],
            axis=0,
        )
        value = ready
        if q < last:
            value = value - across(newest, band_of(q, b + 1, b + 3))
        value = across(parts_of(value), halves(inverse))
        whole_ref[:, pl.ds(a * SIDE, 2 * SIDE)] = value
        newest = parts_of(value)
        known = newest if known is None else jnp.concatenate([newest, known], axis=1)
        if q > 0:
            ready = whole_ref[:, pl.ds((a - 2) * SIDE, 2 * SIDE)]
            if q < last:
                if q - 1 > last // 2:
                    copies[last - q + 1].wait()
                ready = ready - across(known[:, 2 * SIDE:], band_of(q - 1, b + 1, count))
    mine = pl.ds(pl.multiple_of(where_ref[1] * SIDE, SIDE), SIDE)
    solved_ref[...] = whole_ref[:, mine]
    rest_copy.wait()
    top_copy.wait()


def final_of(where, own, other, summit, back, reflect, rotated, folded):
    columns = summit.shape[0]
    order = reflect.shape[1]
    rows, near, long = folded.shape[:3]
    narrow = own.shape[1] - SIDE
    hbm = pl.BlockSpec(memory_space=pltpu.HBM)
    return pl.pallas_call(
        final_kernel,
        in_specs=[smem] + [vmem] * 5 + [hbm] * 2,
        out_specs=[hbm, vmem],
        out_shape=[shaped(*rotated.shape), shaped(narrow, SIDE)],
        scratch_shapes=[
            pltpu.VMEM((order, columns), jnp.float32),
            pltpu.VMEM((narrow, order), jnp.float32),
            pltpu.VMEM((SIDE, columns), jnp.float32),
            pltpu.VMEM((near // 2, rows, 2, long) + folded.shape[3:], jnp.float32),
            pltpu.SemaphoreType.DMA((near // 2,)),
            pltpu.SemaphoreType.DMA((2,)),
        ],
        compiler_params=params(LARGE),
        cost_estimate=cost(8 * columns * order * order, 4 * folded.size),
        name="final",
    )(where, own, other, summit, back, reflect, rotated, folded)


def dot(left, right):
    return jnp.dot(left, right, precision=lax.Precision.HIGHEST, preferred_element_type=jnp.float32)


def moved(value, axis, pairs):
    return lax.ppermute(value, axis, pairs)


def per_device(
    right_side, reflectors, leaf_factor, node_reflect, node_factor, upper_blocks, block_inverse
):
    block = upper_blocks.shape[0]
    columns = right_side.shape[1]
    count = lax.axis_size("leaf")
    rows = lax.axis_size("rows")
    half = count // 2
    row_index = lax.axis_index("rows")
    leaf_index = lax.axis_index("leaf")
    where = jnp.stack([leaf_index % 2, leaf_index, row_index]).astype(jnp.int32)
    swap = [(i, i ^ 1) for i in range(count)]
    same = [list(range(k, count, 2)) for k in range(2)]

    def pair_sum(parts):
        keep, give = parts
        return keep + moved(give, "leaf", swap)

    def scatter_pair(pair):
        got = lax.all_to_all(pair, "leaf", 0, 0, axis_index_groups=same)
        return jnp.sum(got, axis=0)

    def copies(mine):
        return jnp.broadcast_to(mine[None], (half,) + mine.shape)

    def collect(spread):
        own = lax.all_to_all(spread, "leaf", 0, 0, axis_index_groups=same)
        return own, moved(own, "leaf", swap)

    start = KEPT * block
    longest = moved(
        node_factor[0, start:], "leaf", [(k, ENDS[k][0]) for k in (14, 15)]
    )
    longer = moved(
        node_factor[0, start:start + 4 * block], "leaf", [(k, ENDS[k][0]) for k in (10, 11, 12, 13)]
    )
    keep, give = weights_of(where, right_side, reflectors)
    keep, longest, longer = lax.optimization_barrier((keep, longest, longer))

    def lowered_by(value, first):
        return jnp.pad(value, ((first * block, start - first * block - value.shape[0]), (0, 0)))

    longer = jnp.where(
        leaf_index < ENDS[10][0],
        lowered_by(longer, ENDS[12][1]),
        lowered_by(longer[:2 * block], ENDS[10][1]),
    )
    factor_whole = lax.all_gather(
        node_factor[0, :start] + (lowered_by(longest, ENDS[14][1]) + longer), "leaf", axis=0
    )
    weights_part = scatter_pair(pair_sum((keep, give)))
    spread = coeffs_of(where, *collect(copies(weights_part)), leaf_factor[0])
    rotated, top = lowered_of(where, *collect(spread), reflectors, right_side)

    upper_own, inverse_own = upper_blocks, block_inverse
    inverse_next = moved(inverse_own, "leaf", [(i + 1, i) for i in range(0, count, 2)])
    eighth = block // rows
    upper_slice = lax.dynamic_slice_in_dim(upper_own, row_index * eighth, eighth, 0)
    inverse_slice = lax.dynamic_slice_in_dim(inverse_own, row_index * eighth, eighth, 0)
    upper_slice = upper_slice.reshape(eighth, count, block).transpose(1, 0, 2)
    beside = lax.dynamic_slice_in_dim(
        upper_own, jnp.minimum(leaf_index + 1, count - 1) * block, block, 1
    )
    cross = dot(dot(inverse_slice, beside), inverse_next)
    at_cross = jnp.arange(count)[:, None, None] == leaf_index + 1
    at_cross = jnp.logical_and(at_cross, leaf_index % 2 == 0)
    upper_slice = jnp.where(at_cross, cross[None], upper_slice)
    upper_slice = jnp.concatenate([upper_slice, inverse_slice[None]], axis=0)

    joint = joint_of(where, node_reflect[0], factor_whole)

    stride = 1
    upper = top
    lower = moved(top, "rows", [(i, i + 1) for i in range(0, rows, 2)])
    own_coeffs = jnp.zeros_like(top)
    own_top = top
    while stride < rows:
        if stride > 1:
            nodes = list(range(stride, rows, 2 * stride))
            upper = moved(lower, "rows", [(j + stride // 2, j) for j in nodes])
            lower = moved(lower, "rows", [(j - stride // 2, j) for j in nodes])
        if stride == 4:
            upper, lower, folded = lax.optimization_barrier((upper, lower, folded))
            folded = lax.all_gather(folded, "rows", axis=0)
        parts = level_of(where, upper, lower, joint)
        if stride == 1:
            upper_slice, parts = lax.optimization_barrier((upper_slice, parts))
            pieces = lax.all_gather(upper_slice, "leaf", axis=0)
        share = scatter_pair(pair_sum(parts))
        if stride == 2:
            folded = fold_of(pieces, share)
        lower = lower - share
        mine = row_index % (2 * stride) == stride
        own_coeffs = jnp.where(mine, share, own_coeffs)
        own_top = jnp.where(mine, upper, own_top)
        stride *= 2
    root = rows // 2

    back = moved(lower, "rows", [(root, 0)])
    pieces = lower.reshape(rows, columns // rows, block)
    arrived = lax.all_to_all(pieces, "rows", 0, 0)[root]
    arrived, back = lax.optimization_barrier((arrived, back))
    own, other = collect(copies(jnp.concatenate([own_coeffs.T, arrived], axis=0)))
    rotated, solved = final_of(
        where, own, other, own_top, back, node_reflect[0], rotated, folded
    )
    return (rotated, solved.T)


def solution(mesh):
    in_specs = (
        P(("rows", "leaf"), None),
        P(("rows", "leaf"), None),
        P("rows", None, "leaf"),
        P("rows", "leaf", None),
        P("rows", None, "leaf"),
        P("leaf", None),
        P("leaf", None),
    )
    out_specs = (P(("rows", "leaf"), None), P("leaf", "rows"))
    return jax.shard_map(
        per_device, mesh=mesh, in_specs=in_specs, out_specs=out_specs, check_vma=False
    )
```

```python
import functools

import jax
import jax.numpy as jnp
from jax import lax
from jax.experimental import pallas as pl
from jax.experimental.pallas import tpu as pltpu
from jax.sharding import PartitionSpec as P

SIDE = 128
GROUP = 4
SPLIT = (((1,), (0,)), ((), ()))
SMALL = 24 * 1024 * 1024
MEDIUM = 51 * 1024 * 1024
LARGE = 56 * 1024 * 1024


def halves(value):
    high = value.astype(jnp.bfloat16)
    low = (value - high.astype(jnp.float32)).astype(jnp.bfloat16)
    return high, low


def once(left, right):
    return lax.dot_general(left, right, SPLIT, preferred_element_type=jnp.float32)


def crossed(left, right):
    return lax.dot_general(
        left, right, (((1,), (1,)), ((), ())), preferred_element_type=jnp.float32
    )


def thrice(left, right):
    return once(left[0], right[0]) + (once(left[0], right[1]) + once(left[1], right[0]))


def stacked(left, right):
    size = left[0].shape[0]
    both = once(jnp.concatenate(left, axis=0), right[0])
    return both[:size] + (both[size:] + once(left[0], right[1]))


def pick(parity, own, other):
    first = parity == 0
    return jnp.where(first, own, other), jnp.where(first, other, own)


smem = pl.BlockSpec(memory_space=pltpu.SMEM)


vmem = pl.BlockSpec(memory_space=pltpu.VMEM)


def params(limit=SMALL):
    return pltpu.CompilerParams(vmem_limit_bytes=limit)


def cost(flops, size):
    return pl.CostEstimate(flops=flops, bytes_accessed=size, transcendentals=0)


def shaped(*shape, dtype=jnp.float32):
    return jax.ShapeDtypeStruct(shape, dtype)


def weights_kernel(where_ref, side_ref, vectors_ref, keep_ref, give_ref, high_ref, low_ref):
    @pl.when(pl.program_id(0) == 0)
    def _():
        high, low = halves(side_ref[...].T)
        high_ref[...] = high
        low_ref[...] = low

    first = where_ref[0] == 0
    for n in range(keep_ref.shape[0]):
        vectors = vectors_ref[:, 2 * n * SIDE:(2 * n + 2) * SIDE]
        out = stacked((high_ref[...], low_ref[...]), halves(vectors))
        even, odd = out[:, :SIDE], out[:, SIDE:]
        keep_ref[n] = jnp.where(first, even, odd)
        give_ref[n] = jnp.where(first, odd, even)


def weights_of(where, side, vectors):
    tall, order = vectors.shape
    columns = side.shape[1]
    steps = order // (2 * SIDE)
    block = pl.BlockSpec((GROUP, columns, SIDE), lambda n: (n, 0, 0))
    return pl.pallas_call(
        weights_kernel,
        grid=(steps // GROUP,),
        in_specs=[
            smem,
            pl.BlockSpec((tall, columns), lambda n: (0, 0)),
            pl.BlockSpec((tall, 2 * GROUP * SIDE), lambda n: (0, n)),
        ],
        out_specs=[block, block],
        out_shape=[shaped(steps, columns, SIDE)] * 2,
        scratch_shapes=[pltpu.VMEM((columns, tall), jnp.bfloat16)] * 2,
        compiler_params=params(LARGE),
        cost_estimate=cost(6 * tall * columns * order, 4 * vectors.size),
        name="weights",
    )(where, side, vectors)


def coeffs_kernel(where_ref, own_ref, other_ref, factor_ref, out_ref):
    parity = where_ref[0]
    steps = own_ref.shape[0]
    total = jnp.zeros(own_ref.shape[1:], jnp.float32)
    for n in range(steps):
        left = jnp.concatenate(pick(parity, own_ref[n], other_ref[n]), axis=1)
        right = factor_ref[2 * n * SIDE:(2 * n + 2) * SIDE, :]
        total = total + stacked(halves(left), halves(right))
    total = total.T
    for n in range(steps):
        out_ref[n] = total


def coeffs_of(where, own, other, factor):
    return pl.pallas_call(
        coeffs_kernel,
        in_specs=[smem] + [pl.BlockSpec(memory_space=pltpu.VMEM)] * 3,
        out_shape=shaped(own.shape[0], SIDE, own.shape[1]),
        compiler_params=params(),
        cost_estimate=cost(6 * own.shape[1] * factor.size, 4 * factor.size),
        name="coeffs",
    )(where, own, other, factor)


def lowered_step(step, where_ref, own_ref, other_ref, vectors_ref, side_ref, sum_ref):
    @pl.when(step == 0)
    def _():
        sum_ref[...] = side_ref[...]

    total = sum_ref[...]
    for n in range(own_ref.shape[0]):
        right = jnp.concatenate(pick(where_ref[0], own_ref[n], other_ref[n]), axis=0)
        vectors = vectors_ref[:, 2 * n * SIDE:(2 * n + 2) * SIDE]
        total = total - stacked(halves(vectors), halves(right))
    sum_ref[...] = total


def top_kernel(where_ref, own_ref, other_ref, vectors_ref, side_ref, top_ref, sum_ref):
    step = pl.program_id(1)
    lowered_step(step, where_ref, own_ref, other_ref, vectors_ref, side_ref, sum_ref)

    @pl.when(step == pl.num_programs(1) - 1)
    def _():
        top_ref[...] = sum_ref[...].T


def rest_kernel(where_ref, own_ref, other_ref, vectors_ref, side_ref, out_ref):
    step = pl.program_id(1)
    lowered_step(step, where_ref, own_ref, other_ref, vectors_ref, side_ref, out_ref)


def lowered_of(where, own, other, vectors, side, first, blocks):
    order = vectors.shape[1]
    columns = side.shape[1]
    steps = order // (2 * SIDE)
    block = pl.BlockSpec((GROUP, SIDE, columns), lambda i, n: (n, 0, 0))
    return pl.pallas_call(
        rest_kernel if first else top_kernel,
        grid=(blocks, steps // GROUP),
        in_specs=[
            smem,
            block,
            block,
            pl.BlockSpec((SIDE, 2 * GROUP * SIDE), lambda i, n: (first + i, n)),
            pl.BlockSpec((SIDE, columns), lambda i, n: (first + i, 0)),
        ],
        out_specs=pl.BlockSpec((SIDE, columns), lambda i, n: (i, 0)),
        out_shape=shaped(blocks * SIDE, columns),
        scratch_shapes=[] if first else [pltpu.VMEM((SIDE, columns), jnp.float32)],
        compiler_params=params(LARGE),
        cost_estimate=cost(6 * blocks * SIDE * columns * order, 4 * blocks * SIDE * order),
        name="lowered_rest" if first else "lowered_top",
    )(where, own, other, vectors, side)


KEPT = 10
ENDS = {10: (6, 8), 11: (7, 8), 12: (4, 6), 13: (5, 6), 14: (0, 4), 15: (1, 4)}


def joint_kernel(where_ref, reflect_ref, factor_ref, high_ref, low_ref, panel_ref, sems):
    count, kept, _ = factor_ref.shape
    copies = [None] * count
    for k in reversed(range(count)):
        edge = (k // 2 + 1) * 2 * SIDE
        rows = pl.ds(0, min(edge, kept))
        copies[k] = [
            pltpu.make_async_copy(factor_ref.at[k, rows], panel_ref.at[k, rows], sems.at[0, k])
        ]
        if edge > kept:
            slot, first = ENDS[k]
            copies[k].append(
                pltpu.make_async_copy(
                    factor_ref.at[slot, pl.ds(first * SIDE, edge - kept)],
                    panel_ref.at[k, pl.ds(kept, edge - kept)],
                    sems.at[1, k],
                )
            )
        for copy in copies[k]:
            copy.start()
    reflect = halves(reflect_ref[...])
    own = where_ref[1]
    zero = jnp.zeros((SIDE, SIDE), jnp.float32)
    for k in reversed(range(0, count, 2)):
        for copy in copies[k] + copies[k + 1]:
            copy.wait()
        edge = (k + 2) * SIDE
        panel = jnp.concatenate([panel_ref[k, 0:edge], panel_ref[k + 1, 0:edge]], axis=1)
        top = stacked([r[:, :edge] for r in reflect], halves(panel))
        mine = pl.ds(pl.multiple_of(jnp.minimum(own, k + 1) * SIDE, SIDE), SIDE)
        bottom = [jnp.where(own <= j, panel_ref[j, mine, :], zero) for j in (k, k + 1)]
        bottom = jnp.concatenate(bottom, axis=1)
        at = pl.ds(k * SIDE, 2 * SIDE)
        for ref, first, second in zip((high_ref, low_ref), halves(top), halves(bottom)):
            ref[0:SIDE, at] = first
            ref[SIDE:2 * SIDE, at] = second


def joint_of(where, reflect, factor):
    block, order = reflect.shape
    count = factor.shape[0]
    return pl.pallas_call(
        joint_kernel,
        in_specs=[smem, vmem, pl.BlockSpec(memory_space=pltpu.HBM)],
        out_specs=[vmem] * 2,
        out_shape=[shaped(2 * block, order, dtype=jnp.bfloat16)] * 2,
        scratch_shapes=[
            pltpu.VMEM((count, order, SIDE), jnp.float32),
            pltpu.SemaphoreType.DMA((2, count)),
        ],
        compiler_params=params(MEDIUM),
        cost_estimate=cost(3 * block * order * order, 2 * factor.size),
        name="joint",
    )(where, reflect, factor)


def level_kernel(where_ref, upper_ref, lower_ref, high_ref, low_ref, keep_ref, give_ref):
    first = where_ref[0] == 0
    left = halves(jnp.concatenate([upper_ref[...], lower_ref[...]], axis=1))
    for n in range(keep_ref.shape[0]):
        at = pl.ds(2 * n * SIDE, 2 * SIDE)
        out = stacked(left, (high_ref[:, at], low_ref[:, at]))
        even, odd = out[:, :SIDE], out[:, SIDE:]
        keep_ref[n] = jnp.where(first, even, odd)
        give_ref[n] = jnp.where(first, odd, even)


def level_of(where, upper, lower, joint):
    columns = upper.shape[0]
    wide, order = joint[0].shape
    steps = order // (2 * SIDE)
    return pl.pallas_call(
        level_kernel,
        in_specs=[smem] + [vmem] * 4,
        out_specs=[vmem] * 2,
        out_shape=[shaped(steps, columns, SIDE)] * 2,
        compiler_params=params(),
        cost_estimate=cost(6 * columns * wide * order, 4 * wide * order),
        name="level",
    )(where, upper, lower, *joint)


def fold_kernel(pieces_ref, after_ref, out_ref):
    count = pieces_ref.shape[0]
    for n in range(count // 2):
        far = count - 1 - n
        out_ref[n, 0:far] = pieces_ref[n, n + 1:count]
        out_ref[n, far] = pieces_ref[n, count]
        for k in range(far + 1, count):
            out_ref[n, k] = pieces_ref[far, k]
        out_ref[n, count] = pieces_ref[far, count]


def fold_of(pieces, after):
    count = pieces.shape[0]
    return pl.pallas_call(
        fold_kernel,
        in_specs=[vmem, vmem],
        out_specs=vmem,
        out_shape=shaped(count // 2, *pieces.shape[1:]),
        compiler_params=params(),
        name="fold",
    )(pieces, after)


def final_kernel(
    where_ref, own_ref, other_ref, summit_ref, back_ref, reflect_ref, rotated_ref, folded_ref,
    out_ref, solved_ref, coeffs_ref, whole_ref, top_ref, panel_ref, sems, out_sems,
):
    parity = where_ref[0]
    steps = own_ref.shape[0]
    count = 2 * steps
    copies = []
    for p in range(count // 4):
        copy = pltpu.make_async_copy(
            folded_ref.at[:, 2 * p:2 * p + 2], panel_ref.at[p], sems.at[p]
        )
        copy.start()
        copies.append(copy)
    rest = pl.ds(SIDE, rotated_ref.shape[0])
    rest_copy = pltpu.make_async_copy(rotated_ref, out_ref.at[rest], out_sems.at[0])
    rest_copy.start()
    for n in range(steps):
        for k, value in enumerate(pick(parity, own_ref[n], other_ref[n])):
            at = pl.ds((2 * n + k) * SIDE, SIDE)
            coeffs_ref[at, :] = value[:SIDE]
            whole_ref[:, at] = value[SIDE:]
    lowered = thrice(halves(reflect_ref[...]), halves(coeffs_ref[...]))
    lowered = jnp.where(where_ref[2] == 0, back_ref[...], summit_ref[...] - lowered.T)
    top_ref[...] = lowered.T
    top_copy = pltpu.make_async_copy(top_ref, out_ref.at[0:SIDE], out_sems.at[1])
    top_copy.start()

    def block_at(row, column):
        near = min(row, count - 1 - row)
        if row >= count // 2:
            at = column
        else:
            at = count - 1 - row if column == count else column - row - 1
        return panel_ref[near // 2, :, near % 2, at].reshape(SIDE, SIDE)

    zero = jnp.zeros((SIDE, SIDE), jnp.float32)

    def band_of(q, start, stop):
        bands = [
            jnp.concatenate([block_at(k, j) for j in range(start, stop)], axis=1)
            for k in (2 * q, 2 * q + 1)
        ]
        return halves(jnp.concatenate(bands, axis=0))

    def parts_of(value):
        high = value.astype(jnp.bfloat16).astype(jnp.float32)
        return jnp.concatenate([high, value - high], axis=0).astype(jnp.bfloat16)

    def across(parts, right):
        both = crossed(parts, right[0]) + crossed(parts, right[1])
        size = both.shape[0] // 2
        return both[:size] + both[size:]

    last = count // 2 - 1
    known = None
    ready = whole_ref[:, pl.ds(2 * last * SIDE, 2 * SIDE)]
    for q in reversed(range(last + 1)):
        a, b = 2 * q, 2 * q + 1
        if q == last:
            copies[0].wait()
            copies[1].wait()
        inverse = jnp.concatenate(
            [
                jnp.concatenate([block_at(a, count), -block_at(a, b)], axis=1),
                jnp.concatenate([zero, block_at(b, count)], axis=1),
            ],
            axis=0,
        )
        value = ready
        if q < last:
            value = value - across(newest, band_of(q, b + 1, b + 3))
        value = across(parts_of(value), halves(inverse))
        whole_ref[:, pl.ds(a * SIDE, 2 * SIDE)] = value
        newest = parts_of(value)
        known = newest if known is None else jnp.concatenate([newest, known], axis=1)
        if q > 0:
            ready = whole_ref[:, pl.ds((a - 2) * SIDE, 2 * SIDE)]
            if q < last:
                if q - 1 > last // 2:
                    copies[last - q + 1].wait()
                ready = ready - across(known[:, 2 * SIDE:], band_of(q - 1, b + 1, count))
    mine = pl.ds(pl.multiple_of(where_ref[1] * SIDE, SIDE), SIDE)
    solved_ref[...] = whole_ref[:, mine]
    rest_copy.wait()
    top_copy.wait()


def final_of(where, own, other, summit, back, reflect, rotated, folded):
    columns = summit.shape[0]
    order = reflect.shape[1]
    rows, near, long = folded.shape[:3]
    narrow = own.shape[1] - SIDE
    hbm = pl.BlockSpec(memory_space=pltpu.HBM)
    return pl.pallas_call(
        final_kernel,
        in_specs=[smem] + [vmem] * 5 + [hbm] * 2,
        out_specs=[hbm, vmem],
        out_shape=[shaped(rotated.shape[0] + SIDE, columns), shaped(narrow, SIDE)],
        scratch_shapes=[
            pltpu.VMEM((order, columns), jnp.float32),
            pltpu.VMEM((narrow, order), jnp.float32),
            pltpu.VMEM((SIDE, columns), jnp.float32),
            pltpu.VMEM((near // 2, rows, 2, long) + folded.shape[3:], jnp.float32),
            pltpu.SemaphoreType.DMA((near // 2,)),
            pltpu.SemaphoreType.DMA((2,)),
        ],
        compiler_params=params(LARGE),
        cost_estimate=cost(8 * columns * order * order, 4 * folded.size),
        name="final",
    )(where, own, other, summit, back, reflect, rotated, folded)


def dot(left, right):
    return jnp.dot(left, right, precision=lax.Precision.HIGHEST, preferred_element_type=jnp.float32)


def moved(value, axis, pairs):
    return lax.ppermute(value, axis, pairs)


def per_device(
    right_side, reflectors, leaf_factor, node_reflect, node_factor, upper_blocks, block_inverse
):
    block = upper_blocks.shape[0]
    columns = right_side.shape[1]
    count = lax.axis_size("leaf")
    rows = lax.axis_size("rows")
    half = count // 2
    row_index = lax.axis_index("rows")
    leaf_index = lax.axis_index("leaf")
    where = jnp.stack([leaf_index % 2, leaf_index, row_index]).astype(jnp.int32)
    swap = [(i, i ^ 1) for i in range(count)]
    same = [list(range(k, count, 2)) for k in range(2)]

    def pair_sum(parts):
        keep, give = parts
        return keep + moved(give, "leaf", swap)

    def scatter_pair(pair):
        got = lax.all_to_all(pair, "leaf", 0, 0, axis_index_groups=same)
        return jnp.sum(got, axis=0)

    def copies(mine):
        return jnp.broadcast_to(mine[None], (half,) + mine.shape)

    def collect(spread):
        own = lax.all_to_all(spread, "leaf", 0, 0, axis_index_groups=same)
        return own, moved(own, "leaf", swap)

    start = KEPT * block
    longest = moved(
        node_factor[0, start:], "leaf", [(k, ENDS[k][0]) for k in (14, 15)]
    )
    longer = moved(
        node_factor[0, start:start + 4 * block], "leaf", [(k, ENDS[k][0]) for k in (10, 11, 12, 13)]
    )
    keep, give = weights_of(where, right_side, reflectors)
    keep, longest, longer = lax.optimization_barrier((keep, longest, longer))

    def lowered_by(value, first):
        return jnp.pad(value, ((first * block, start - first * block - value.shape[0]), (0, 0)))

    longer = jnp.where(
        leaf_index < ENDS[10][0],
        lowered_by(longer, ENDS[12][1]),
        lowered_by(longer[:2 * block], ENDS[10][1]),
    )
    factor_whole = lax.all_gather(
        node_factor[0, :start] + (lowered_by(longest, ENDS[14][1]) + longer), "leaf", axis=0
    )
    weights_part = scatter_pair(pair_sum((keep, give)))
    spread = coeffs_of(where, *collect(copies(weights_part)), leaf_factor[0])
    coeffs = collect(spread)
    top = lowered_of(where, *coeffs, reflectors, right_side, 0, 1)
    rest = lowered_of(where, *coeffs, reflectors, right_side, 1, right_side.shape[0] // block - 1)

    upper_own, inverse_own = upper_blocks, block_inverse
    inverse_next = moved(inverse_own, "leaf", [(i + 1, i) for i in range(0, count, 2)])
    eighth = block // rows
    upper_slice = lax.dynamic_slice_in_dim(upper_own, row_index * eighth, eighth, 0)
    inverse_slice = lax.dynamic_slice_in_dim(inverse_own, row_index * eighth, eighth, 0)
    upper_slice = upper_slice.reshape(eighth, count, block).transpose(1, 0, 2)
    beside = lax.dynamic_slice_in_dim(
        upper_own, jnp.minimum(leaf_index + 1, count - 1) * block, block, 1
    )
    cross = dot(dot(inverse_slice, beside), inverse_next)
    at_cross = jnp.arange(count)[:, None, None] == leaf_index + 1
    at_cross = jnp.logical_and(at_cross, leaf_index % 2 == 0)
    upper_slice = jnp.where(at_cross, cross[None], upper_slice)
    upper_slice = jnp.concatenate([upper_slice, inverse_slice[None]], axis=0)

    joint = joint_of(where, node_reflect[0], factor_whole)

    stride = 1
    upper = top
    lower = moved(top, "rows", [(i, i + 1) for i in range(0, rows, 2)])
    own_coeffs = jnp.zeros_like(top)
    own_top = top
    while stride < rows:
        if stride > 1:
            nodes = list(range(stride, rows, 2 * stride))
            upper = moved(lower, "rows", [(j + stride // 2, j) for j in nodes])
            lower = moved(lower, "rows", [(j - stride // 2, j) for j in nodes])
        if stride == 4:
            upper, lower, folded = lax.optimization_barrier((upper, lower, folded))
            folded = lax.all_gather(folded, "rows", axis=0)
        if 2 * stride == rows:
            upper, lower, rest = lax.optimization_barrier((upper, lower, rest))
        parts = level_of(where, upper, lower, joint)
        if stride == 1:
            upper_slice, parts = lax.optimization_barrier((upper_slice, parts))
            pieces = lax.all_gather(upper_slice, "leaf", axis=0)
        share = scatter_pair(pair_sum(parts))
        if stride == 2:
            folded = fold_of(pieces, share)
        lower = lower - share
        mine = row_index % (2 * stride) == stride
        own_coeffs = jnp.where(mine, share, own_coeffs)
        own_top = jnp.where(mine, upper, own_top)
        stride *= 2
    root = rows // 2

    back = moved(lower, "rows", [(root, 0)])
    pieces = lower.reshape(rows, columns // rows, block)
    arrived = lax.all_to_all(pieces, "rows", 0, 0)[root]
    arrived, back = lax.optimization_barrier((arrived, back))
    own, other = collect(copies(jnp.concatenate([own_coeffs.T, arrived], axis=0)))
    rotated, solved = final_of(
        where, own, other, own_top, back, node_reflect[0], rest, folded
    )
    return (rotated, solved.T)


def solution(mesh):
    in_specs = (
        P(("rows", "leaf"), None),
        P(("rows", "leaf"), None),
        P("rows", None, "leaf"),
        P("rows", "leaf", None),
        P("rows", None, "leaf"),
        P("leaf", None),
        P("leaf", None),
    )
    out_specs = (P(("rows", "leaf"), None), P("leaf", "rows"))
    return jax.shard_map(
        per_device, mesh=mesh, in_specs=in_specs, out_specs=out_specs, check_vma=False
    )
```
